32 devices in a mesh: group: 2 (over x), tp: 16 (over z, y, core).
Axes of the slice: x: 2, y: 2, z: 4, core: 2. Of those that a mesh axis runs over, the one named last changes fastest.
Arguments:
- states: bfloat16 [2048, 7168], P(('group', 'tp')), parts along dimension 0, may hold values from -6 to 6
- norm_gain: float32 [7168], replicated, may hold values from 0.1 to 1.9
- w_gate: bfloat16 [7168, 4096], P(None, 'tp'), may hold values from -0.0625 to 0.0625
- w_up: bfloat16 [7168, 4096], P(None, 'tp'), may hold values from -0.0625 to 0.0625
- w_down: bfloat16 [4096, 7168], P('tp'), may hold values from -0.125 to 0.125
- expert_ids: int32 [2048, 8], P(('group', 'tp')), parts along dimension 0, may hold values from 0 to 255, as said below
- gate_weights: float32 [2048, 8], P(('group', 'tp')), parts along dimension 0, may hold values from 0.2 to 2
Outputs:
- routed: bfloat16 [2048, 7168], P(('group', 'tp')), parts along dimension 0
The draws below stay inside these ranges and needn't reach their ends.
There are 2 independent parts, one for each index of `group`. The reference program is written for one: setup_inputs(seed, part) draws one part's arguments, and reference() takes and returns one part's arrays. A program takes and returns all parts, laid end to end along the dimension named above; an argument that names none is the same for every part. Nothing has to cross between parts.
Inputs may be any that keep to these rules, and one draw needn't show every extreme that they name: `expert_ids`: each row names 8 different experts, two from each of 4 different nodes, the node of an expert being its id divided by 32. Among the rows of one device, each expert k * 32 with k < 2 is named by at least one and at most 8 rows, and in every draw one of these experts is named by exactly 8 rows of every device. No row names more than two of these experts.
All inputs are finite; a program needn't handle non-finite values.
Results may differ from the reference program's by a relative error of at most 0.007.
Values may be sent and summed in bfloat16 or wider, within the bound.
No kernel may reach another device: no remote copies, remote signals or barrier semaphores. Data moves between devices by JAX's collectives and lax.ppermute only.
A program may use at most 128 MiB of HBM per device.

```python
import math
import jax
import jax.numpy as jnp
from jax import lax

D = 7168
HID = 2048
EXPERTS = 256
TOPK = 8
NODES = 8
NODE_TOP = 4
SPLIT = 8
CAP = 8
TOK_DEV = 64
WAVE = 2
TOKENS = 1024
N_TP = 16


def draw_expert_ids(key, part):
    key = jax.random.fold_in(key, 11)
    blocks = TOKENS // TOK_DEV
    per_node = EXPERTS // NODES
    subkeys = jax.random.split(key, 9)
    weights = jax.random.randint(subkeys[0], (WAVE,), 1, 5)
    counts = jnp.minimum(CAP, 1 + jax.random.randint(subkeys[1], (blocks, WAVE), 0, CAP) * weights[None, :] // 4)
    hottest = jax.random.randint(subkeys[2], (), 0, WAVE)
    counts = jnp.where(jnp.arange(WAVE)[None, :] == hottest, CAP, counts)
    scores = jax.random.randint(subkeys[3], (blocks, TOK_DEV), 0, 65536) * TOK_DEV + jnp.arange(TOK_DEV)[None, :]
    rank_of = jnp.argsort(jnp.argsort(scores, axis=1), axis=1)
    spacing = CAP // 2
    offsets = (rank_of[:, :, None] - jnp.arange(WAVE)[None, None, :] * spacing) % TOK_DEV
    hit_rows = (offsets < counts[:, None, :]).reshape(TOKENS, WAVE).astype(jnp.int32)
    hit_nodes = jnp.concatenate([hit_rows, jnp.zeros((TOKENS, NODES - WAVE), jnp.int32)], axis=1)
    node_scores = jax.random.randint(subkeys[4], (TOKENS, NODES), 0, 1024) * NODES + jnp.arange(NODES)[None, :] + hit_nodes * 1048576
    top_scores, chosen = lax.top_k(node_scores, NODE_TOP)
    shuffle = jnp.argsort(jax.random.randint(subkeys[5], (TOKENS, NODE_TOP), 0, 1024) * NODE_TOP + jnp.arange(NODE_TOP)[None, :], axis=1)
    chosen = jnp.take_along_axis(chosen, shuffle, axis=1)
    chosen_hit = jnp.take_along_axis(hit_nodes, chosen, axis=1)
    first_off = jax.random.randint(subkeys[6], (TOKENS, NODE_TOP), 1, per_node)
    second = 1 + (first_off - 1 + jax.random.randint(subkeys[7], (TOKENS, NODE_TOP), 1, per_node - 1)) % (per_node - 1)
    first_off = jnp.where(chosen_hit == 1, 0, first_off)
    swapped = jax.random.randint(subkeys[8], (TOKENS, NODE_TOP), 0, 2) == 1
    left_off = jnp.where(swapped, second, first_off)
    right_off = jnp.where(swapped, first_off, second)
    picked = jnp.stack([chosen * per_node + left_off, chosen * per_node + right_off], axis=2)
    return picked.reshape(TOKENS, NODE_TOP * 2).astype(jnp.int32)


def shard_levels(own_key, shape, cuts, least, top_value):
    def one(axis_at, parts):
        steps = jax.random.uniform(jax.random.fold_in(jax.random.fold_in(own_key, 6), axis_at), (parts,), jnp.float32, least / len(cuts), top_value / len(cuts))
        return jnp.repeat(jnp.exp(steps), shape[axis_at] // parts).reshape((-1,) + (1,) * (len(shape) - axis_at - 1))

    loudness = one(*cuts[0])
    for cut in cuts[1:]:
        loudness = loudness * one(*cut)
    return loudness


def centred(stream_key, shape, scale, most, shards=(), held_as=jnp.bfloat16):
    values = scale * jax.random.normal(stream_key, shape, jnp.float32)
    if shards:
        values = values * shard_levels(stream_key, shape, shards, -0.22, 0.18)
    return jnp.clip(values, -most, most).astype(held_as)


def setup_inputs(seed: int = 0, part: int = 0) -> dict:
    seeds = jax.random.split(jax.random.key(seed), 8)
    own_keys = jax.random.split(jax.random.fold_in(seeds[7], part), 8)
    return {
        "states": centred(own_keys[0], (TOKENS, D), 1.0, 6.0, ((0, 16),)),
        "norm_gain": jnp.clip(1.0 + 0.18 * jax.random.normal(seeds[1], (D,), jnp.float32), 0.1, 1.9),
        "w_gate": centred(seeds[2], (D, WAVE * HID), D ** -0.5, 0.0625, ((1, 16),)),
        "w_up": centred(seeds[3], (D, WAVE * HID), D ** -0.5, 0.0625, ((1, 16),)),
        "w_down": centred(seeds[4], (WAVE * HID, D), HID ** -0.5, 0.125, ((0, 16),)),
        "expert_ids": draw_expert_ids(jax.random.fold_in(jax.random.fold_in(seeds[7], part), 71), part),
        "gate_weights": jnp.clip(jnp.exp(math.log(2.0) - 2.3025851 * jax.random.uniform(own_keys[6], (TOKENS, TOPK), jnp.float32) ** shard_levels(own_keys[6], (TOKENS, TOPK), ((0, 16),), -0.2, 0.2)), 0.2, 2.0),
    }


epsilon = 1e-06

def reference(states, norm_gain, w_gate, w_up, w_down, expert_ids, gate_weights):
    hidden_dev = HID // SPLIT
    slot_total = N_TP * CAP
    squares = lax.optimization_barrier(jnp.mean(jnp.square(states.astype(jnp.float32)), axis=1, keepdims=True))
    normed = (states.astype(jnp.float32) * lax.rsqrt(squares + epsilon) * norm_gain).astype(jnp.bfloat16)
    routed = jnp.zeros((TOKENS, D), jnp.float32)
    for expert in range(WAVE):
        matched = expert_ids == expert * (EXPERTS // NODES)
        score = lax.optimization_barrier(jnp.sum(jnp.where(matched, gate_weights, jnp.float32(0.0)), axis=1))
        named = jnp.any(matched, axis=1)
        chosen = jnp.nonzero(named, size=slot_total, fill_value=0)[0].astype(jnp.int32)
        occupied = jnp.arange(slot_total, dtype=jnp.int32) < jnp.sum(named.astype(jnp.int32))
        row_block = normed[chosen]
        first_col = expert * HID
        gated_pre = jnp.dot(row_block, w_gate[:, first_col:first_col + HID], preferred_element_type=jnp.float32)
        up_pre = jnp.dot(row_block, w_up[:, first_col:first_col + HID], preferred_element_type=jnp.float32)
        hidden = (jax.nn.silu(gated_pre) * up_pre).astype(jnp.bfloat16)
        expert_out = jnp.zeros((slot_total, D), jnp.float32)
        for shard_index in range(SPLIT):
            lower_col = shard_index * hidden_dev
            shard_out = jnp.dot(hidden[:, lower_col:lower_col + hidden_dev], w_down[first_col + lower_col:first_col + lower_col + hidden_dev], preferred_element_type=jnp.float32).astype(jnp.bfloat16)
            shard_out = lax.optimization_barrier(shard_out)
            expert_out = expert_out + shard_out.astype(jnp.float32)
        factor = jnp.where(occupied, score[chosen], jnp.float32(0.0))
        routed = routed.at[chosen].add(factor[:, None] * expert_out)
    return routed.astype(jnp.bfloat16)
```

```python
import jax
import jax.numpy as jnp
from jax import lax
from jax.sharding import PartitionSpec as P

EXPERTS = 256
NODES = 8
SPLIT = 8
CAP = 8
EPSILON = 1e-06
SQUARE = (2, 4, 6)


def local(states, norm_gain, w_gate, w_up, w_down, expert_ids, gate_weights):
    width = states.shape[1]
    devices = lax.axis_size("tp")
    waves = devices // SPLIT
    me = lax.axis_index("tp")
    own = me // SPLIT

    def swap(x, mask):
        return lax.ppermute(x, "tp", [(i, i ^ mask) for i in range(devices)])

    targets = (own ^ jnp.arange(waves, dtype=jnp.int32)) * (EXPERTS // NODES)
    matched = expert_ids[:, :, None] == targets[None, None, :]
    score = jnp.sum(jnp.where(matched, gate_weights[:, :, None], 0.0), axis=1)
    hit = jnp.any(matched, axis=1).astype(jnp.int32)
    position = jnp.cumsum(hit, axis=0) - 1
    slots = jnp.arange(CAP, dtype=jnp.int32)
    selector = (hit.T[:, None, :] == 1) & (position.T[:, None, :] == slots[None, :, None])
    rows = jnp.einsum(
        "kct,td->kcd", selector.astype(jnp.bfloat16), states, preferred_element_type=jnp.float32
    )
    squares = jnp.mean(jnp.square(rows), axis=2, keepdims=True)
    packed = (rows * lax.rsqrt(squares + EPSILON) * norm_gain).astype(jnp.bfloat16)
    cross = [SPLIT * j + 4 for j in range(1, waves)]

    blocks = []
    for j in range(waves):
        block = packed[j] if j == 0 else swap(packed[j], cross[j - 1])
        blocks += [block] + [swap(block, s) for s in SQUARE]
    mine = jnp.concatenate(blocks, axis=0)
    theirs = swap(mine, 1)
    both = jnp.concatenate([mine, theirs], axis=0)

    gated = jnp.dot(both, w_gate, preferred_element_type=jnp.float32)
    up = jnp.dot(both, w_up, preferred_element_type=jnp.float32)
    hidden = (jax.nn.silu(gated) * up).astype(jnp.bfloat16)
    half = hidden.shape[0] // 2
    theirs_out = jnp.dot(hidden[half:], w_down, preferred_element_type=jnp.float32).astype(jnp.bfloat16)
    back = swap(theirs_out, 1)
    mine_out = jnp.dot(hidden[:half], w_down, preferred_element_type=jnp.float32)
    pair = (mine_out + back.astype(jnp.float32)).astype(jnp.bfloat16)
    pair = pair.reshape(waves, 1 + len(SQUARE), CAP, width)

    results = [None] * waves
    for j in list(range(1, waves)) + [0]:
        total = pair[j, 0].astype(jnp.float32)
        for n, s in enumerate(SQUARE):
            total = total + swap(pair[j, n + 1], s).astype(jnp.float32)
        if j:
            total = swap(total.astype(jnp.bfloat16), cross[j - 1]).astype(jnp.float32)
        results[j] = total
    summed = jnp.stack(results)
    weighted = jnp.where(selector, score.T[:, None, :], 0.0)
    routed = jnp.einsum("kct,kcd->td", weighted, summed, precision=lax.Precision.HIGHEST)
    return routed.astype(jnp.bfloat16)


def solution(mesh):
    rows = P(("group", "tp"), None)
    in_specs = (rows, P(), P(None, "tp"), P(None, "tp"), P("tp", None), rows, rows)
    return jax.shard_map(local, mesh=mesh, in_specs=in_specs, out_specs=rows, check_vma=False)
```

```python
import functools

import jax
import jax.numpy as jnp
from jax import lax
from jax.experimental import pallas as pl
from jax.experimental.pallas import tpu as pltpu
from jax.sharding import PartitionSpec as P

EXPERTS = 256
NODES = 8
SPLIT = 8
CAP = 8
EPSILON = 1e-06
SQUARE = (2, 4, 6)
F32 = jnp.float32
BF16 = jnp.bfloat16
VMEM = pl.BlockSpec(memory_space=pltpu.VMEM)


def call(body, outs, flops, moved):
    return pl.pallas_call(
        body,
        out_shape=outs,
        compiler_params=pltpu.CompilerParams(vmem_limit_bytes=16 * 1024 * 1024),
        cost_estimate=pl.CostEstimate(flops=flops, bytes_accessed=moved, transcendentals=0),
    )


def normed(picked, states_ref, gain_ref):
    rows = jnp.dot(picked, states_ref[...], preferred_element_type=F32)
    squares = jnp.mean(rows * rows, axis=1, keepdims=True)
    return (rows * lax.rsqrt(squares + EPSILON) * gain_ref[...]).astype(BF16)


def pick_kernel(waves, states_ref, gain_ref, ids_ref, gates_ref, *outs):
    cross_refs, (own_ref, weighted_ref) = outs[:-2], outs[-2:]
    tokens = ids_ref.shape[1]
    own = lax.axis_index("tp") // SPLIT
    upper = lax.broadcasted_iota(jnp.int32, (tokens, tokens), 0)
    upper = (upper <= lax.broadcasted_iota(jnp.int32, (tokens, tokens), 1)).astype(F32).astype(BF16)
    slot = lax.broadcasted_iota(jnp.int32, (CAP, tokens), 0).astype(F32)
    for j in range(waves):
        target = lax.bitwise_xor(own, j) * (EXPERTS // NODES)
        matched = ids_ref[...] == target
        score = jnp.sum(jnp.where(matched, gates_ref[...], 0.0), axis=0, keepdims=True)
        hit = jnp.sum(jnp.where(matched, 1.0, 0.0), axis=0, keepdims=True)
        hits = jnp.broadcast_to(hit, (CAP, tokens))
        place = jnp.dot(hits.astype(BF16), upper, preferred_element_type=F32) - 1.0
        picked = jnp.where((hits > 0.5) & (place == slot), 1.0, 0.0)
        weighted_ref[CAP * j : CAP * (j + 1), :] = picked * score
        if j:
            cross_refs[j - 1][...] = normed(picked.astype(BF16), states_ref, gain_ref)
        else:
            own_ref[...] = picked


def own_kernel(picked_ref, states_ref, gain_ref, out_ref):
    out_ref[...] = normed(picked_ref[...].astype(BF16), states_ref, gain_ref)


def combine_kernel(waves, weighted_ref, *refs):
    pieces, out_ref = refs[:-1], refs[-1]
    own = pieces[0][...].astype(F32)
    for piece in pieces[1 : 1 + len(SQUARE)]:
        own = own + piece[...].astype(F32)
    rows = jnp.concatenate([own] + [p[...].astype(F32) for p in pieces[1 + len(SQUARE) :]], axis=0)
    high = rows.astype(BF16).astype(F32)
    rows = jnp.concatenate([high, high, rows - high], axis=0).astype(BF16)
    weights = weighted_ref[...]
    high = weights.astype(BF16).astype(F32)
    weights = jnp.concatenate([high, weights - high, high], axis=0).astype(BF16)
    out_ref[...] = lax.dot_general(
        weights, rows, (((0,), (0,)), ((), ())), preferred_element_type=F32
    ).astype(BF16)


def local(states, norm_gain, w_gate, w_up, w_down, expert_ids, gate_weights):
    tokens, width = states.shape
    devices = lax.axis_size("tp")
    waves = devices // SPLIT

    def swap(x, mask):
        return lax.ppermute(x, "tp", [(i, i ^ mask) for i in range(devices)])

    block = jax.ShapeDtypeStruct((CAP, width), BF16)
    gain = norm_gain[None, :]
    *cross, picked, weighted = call(
        functools.partial(pick_kernel, waves),
        [block] * (waves - 1)
        + [jax.ShapeDtypeStruct((CAP, tokens), F32), jax.ShapeDtypeStruct((CAP * waves, tokens), F32)],
        2 * tokens * width * CAP * (waves - 1),
        tokens * width * 2,
    )(states, gain, expert_ids.T, gate_weights.T)
    heads = [None] + [swap(x, SPLIT * j + 4) for j, x in enumerate(cross, 1)]
    heads[0] = call(own_kernel, block, 2 * tokens * width * CAP, tokens * width * 2)(picked, states, gain)

    hidden = []
    for j in range(waves):
        mine = jnp.concatenate([heads[j]] + [swap(heads[j], s) for s in SQUARE], axis=0)
        both = jnp.concatenate([mine, swap(mine, 1)], axis=0)
        gated = jnp.dot(both, w_gate, preferred_element_type=F32)
        up = jnp.dot(both, w_up, preferred_element_type=F32)
        hidden.append((jax.nn.silu(gated) * up).astype(BF16))

    results = []
    for j in list(range(1, waves)) + [0]:
        half = hidden[j].shape[0] // 2
        theirs = jnp.dot(hidden[j][half:], w_down, preferred_element_type=F32).astype(BF16)
        back = swap(theirs, 1)
        mine = jnp.dot(hidden[j][:half], w_down, preferred_element_type=F32)
        pair = (mine + back.astype(F32)).astype(BF16)
        parts = [pair[:CAP]] + [swap(pair[CAP * n : CAP * (n + 1)], s) for n, s in enumerate(SQUARE, 1)]
        if j:
            total = parts[0].astype(F32)
            for part in parts[1:]:
                total = total + part.astype(F32)
            results.append(swap(total.astype(BF16), SPLIT * j + 4))
        else:
            results = parts + results
    return call(
        functools.partial(combine_kernel, waves),
        jax.ShapeDtypeStruct((tokens, width), BF16),
        6 * tokens * width * CAP * waves,
        tokens * width * 4,
    )(weighted, *results)


def solution(mesh):
    rows = P(("group", "tp"), None)
    in_specs = (rows, P(), P(None, "tp"), P(None, "tp"), P("tp", None), rows, rows)
    return jax.shard_map(local, mesh=mesh, in_specs=in_specs, out_specs=rows, check_vma=False)
```

```python
import functools

import jax
import jax.numpy as jnp
from jax import lax
from jax.experimental import pallas as pl
from jax.experimental.pallas import tpu as pltpu
from jax.sharding import PartitionSpec as P

EXPERTS = 256
NODES = 8
SPLIT = 8
CAP = 8
EPSILON = 1e-06
SIDES = (2, 4)
CORNER = 6
PICK_LIMIT = 58
OWN_FLOPS = 7_000_000_000
CHUNK = 1024
F32 = jnp.float32
BF16 = jnp.bfloat16


def call(body, outs, args, after=(), far_args=(), scratch=(), flops=0, moved=0, limit=16, out_kind=pltpu.VMEM):
    left, used = len(far_args), len(far_args) + len(args)

    def run(*refs):
        body(*refs[:used], *refs[used + len(after) :])

    def space(kind):
        return pl.BlockSpec(memory_space=kind)

    return pl.pallas_call(
        run,
        out_shape=outs,
        in_specs=[space(pltpu.HBM)] * left + [space(pltpu.VMEM)] * len(args) + [space(pl.ANY)] * len(after),
        out_specs=jax.tree.map(lambda _: space(out_kind), outs),
        scratch_shapes=list(scratch),
        compiler_params=pltpu.CompilerParams(vmem_limit_bytes=limit * 1024 * 1024),
        cost_estimate=pl.CostEstimate(flops=flops, bytes_accessed=moved, transcendentals=0),
    )(*far_args, *args, *after)


def chunks(width):
    return [slice(at, min(at + CHUNK, width)) for at in range(0, width, CHUNK)]


def normed(picked, states_ref, gain_ref):
    rows = jnp.dot(picked, states_ref[...], preferred_element_type=F32)
    squares = jnp.mean(rows * rows, axis=1, keepdims=True)
    return rows * lax.rsqrt(squares + EPSILON) * gain_ref[...]


def pick_kernel(waves, states_hbm, gain_hbm, ids_hbm, gates_hbm, *refs):
    row_refs, weighted_ref = refs[:waves], refs[waves]
    states_ref, gain_ref, ids_ref, gates_ref, sems = refs[waves + 1 :]
    copies = [
        pltpu.make_async_copy(source, target, sems.at[n])
        for n, (source, target) in enumerate(
            [(ids_hbm, ids_ref), (states_hbm, states_ref), (gates_hbm, gates_ref), (gain_hbm, gain_ref)]
        )
    ]
    for copy in copies:
        copy.start()
    tokens = ids_ref.shape[1]
    own = lax.axis_index("tp") // SPLIT
    upper = lax.broadcasted_iota(jnp.int32, (tokens, tokens), 0)
    upper = (upper <= lax.broadcasted_iota(jnp.int32, (tokens, tokens), 1)).astype(F32).astype(BF16)
    slot = lax.broadcasted_iota(jnp.int32, (CAP, tokens), 0).astype(F32)
    copies[0].wait()
    picks = []
    for j in range(waves):
        target = lax.bitwise_xor(own, j) * (EXPERTS // NODES)
        matched = ids_ref[...] == target
        hit = jnp.sum(jnp.where(matched, 1.0, 0.0), axis=0, keepdims=True)
        hits = jnp.broadcast_to(hit, (CAP, tokens))
        place = jnp.dot(hits.astype(BF16), upper, preferred_element_type=F32) - 1.0
        picks.append(jnp.where((hits > 0.5) & (place == slot), 1.0, 0.0))
    for copy in copies[1:]:
        copy.wait()
    for j, picked in enumerate(picks):
        matched = ids_ref[...] == lax.bitwise_xor(own, j) * (EXPERTS // NODES)
        score = jnp.sum(jnp.where(matched, gates_ref[...], 0.0), axis=0, keepdims=True)
        weighted_ref[CAP * j : CAP * (j + 1), :] = picked * score
    rows = normed(jnp.concatenate(picks, axis=0).astype(BF16), states_ref, gain_ref)
    for j, ref in enumerate(row_refs):
        ref[...] = rows[CAP * j : CAP * (j + 1)].astype(BF16)


def copy_kernel(ref, out_ref):
    out_ref[...] = ref[...]


def stack_kernel(*refs):
    for at in chunks(refs[-1].shape[1]):
        parts = [ref[:, at].astype(F32) for ref in refs[:-1]]
        refs[-1][:, at] = jnp.concatenate(parts, axis=0).astype(BF16)


def mark_kernel(ref, out_ref):
    out_ref[...] = ref[:, :128].astype(F32)


def ffn_kernel(gate_ref, up_ref, down_ref, *refs):
    blocks, outs = refs[: len(refs) // 2], refs[len(refs) // 2 :]
    width = blocks[0].shape[1]
    gated = up = 0.0
    for at in chunks(width):
        both = jnp.concatenate([block[:, at].astype(F32) for block in blocks], axis=0).astype(BF16)
        gated += jnp.dot(both, gate_ref[at, :], preferred_element_type=F32)
        up += jnp.dot(both, up_ref[at, :], preferred_element_type=F32)
    hidden = (gated / (1.0 + jnp.exp(-gated)) * up).astype(BF16)
    for at in chunks(width):
        result = jnp.dot(hidden, down_ref[:, at], preferred_element_type=F32)
        first = 0
        for out in outs:
            out[:, at] = result[first : first + out.shape[0]].astype(BF16)
            first += out.shape[0]


def halves(width):
    middle = width // 256 * 128
    return slice(0, middle), slice(middle, width)


def extras(width, blocks, half):
    size = half.stop - half.start
    per = -(-size // (128 * blocks)) * 128
    spans = [(at, min(at + per, size)) for at in range(0, size, per)]
    return [(n, slice(width, width + b - a), slice(half.start + a, half.start + b)) for n, (a, b) in enumerate(spans)]


def message_width(width, blocks):
    return width + max(-(-(h.stop - h.start) // (128 * blocks)) * 128 for h in halves(width))


def rows_of(n):
    return slice(CAP * n, CAP * (n + 1))


def outward_kernel(*refs):
    heads, sides, far_ref, outs = refs[:-5], refs[-5:-3], refs[-3], refs[-2:]
    width = far_ref.shape[1]
    for at in chunks(width):
        far = jnp.concatenate([head[:, at].astype(F32) for head in heads], axis=0).astype(BF16)
        for out in (far_ref,) + outs:
            out[:, at] = far
    for out, side, half in zip(outs, sides[::-1], halves(width)[::-1]):
        parts = extras(width, len(heads), half)
        if len(heads) == 1:
            out[:, parts[0][1]] = side[:, parts[0][2]]
        else:
            size = parts[0][1].stop - width
            held = [side[:, here].astype(F32) for _, _, here in parts]
            held += [jnp.zeros((CAP, size), F32)] * (len(heads) - len(held))
            held = [jnp.pad(x, ((0, 0), (0, size - x.shape[1]))) for x in held]
            out[:, width : width + size] = jnp.concatenate(held, axis=0).astype(BF16)


def arrived_kernel(*refs):
    sides, corner, out_ref = refs[:2], refs[2], refs[3]
    rows, width = corner.shape
    blocks = rows // CAP
    left, right = halves(width)
    corners = {}
    for side, half in zip(sides, (right, left)):
        for n, there, here in extras(width, blocks, half):
            corners[here.start] = (side, n, there)
    edges = sorted(corners)
    for first, last in zip(edges, edges[1:] + [width]):
        for at in chunks(last - first):
            here = slice(first + at.start, first + at.stop)
            side, n, there = corners[first]
            there = slice(there.start + at.start, there.start + at.stop)
            parts = [ref[:, here].astype(F32) for ref in (*sides, corner)]
            parts.append(side[:, there].astype(F32)[rows_of(n)])
            out_ref[:, here] = jnp.concatenate(parts, axis=0).astype(BF16)


def homeward_kernel(home_ref, back_ref, *outs):
    sides, corner = outs[:2], outs[2]
    rows, width = corner.shape
    blocks = rows // CAP
    left, right = halves(width)
    for side, half in zip(sides, (right, left)):
        for n, there, here in extras(width, blocks, half):
            for at in chunks(here.stop - here.start):
                at_here = slice(here.start + at.start, here.start + at.stop)
                at_there = slice(there.start + at.start, there.start + at.stop)
                total = home_ref[:, at_here].astype(F32) + back_ref[:, at_here].astype(F32)
                for k, out in enumerate(outs):
                    out[:, at_here] = total[rows * k : rows * (k + 1)].astype(BF16)
                mine = total[3 * rows :]
                if blocks == 1:
                    side[:, at_there] = mine.astype(BF16)
                else:
                    before = side[:, at_there].astype(F32)
                    pieces = [mine if b == n else before[rows_of(b)] for b in range(blocks)]
                    side[:, at_there] = jnp.concatenate(pieces, axis=0).astype(BF16)


def kept_kernel(skip, home_ref, back_ref, out_ref):
    for at in chunks(home_ref.shape[1]):
        total = home_ref[:, at].astype(F32) + back_ref[:, at].astype(F32)
        out_ref[:, at] = total[skip:]


def total_kernel(*refs):
    arrays, outs = refs[:4], refs[4:]
    for at in chunks(arrays[0].shape[1]):
        total = sum(ref[:, at].astype(F32) for ref in arrays)
        for n, out in enumerate(outs):
            out[:, at] = total[rows_of(n)].astype(BF16)


def near_kernel(home_ref, back_ref, side_one, side_two, kept_ref, one_ref, two_ref):
    width = home_ref.shape[1]
    blocks = side_one.shape[0] // CAP
    left, right = halves(width)
    outs = (one_ref, two_ref)
    for side, half, passed in ((side_two, left, 0), (side_one, right, 1)):
        for n, there, here in extras(width, blocks, half):
            total = home_ref[:, here].astype(F32) + back_ref[:, here].astype(F32)
            kept_ref[:, here] = total[rows_of(0)]
            more = side[:, there].astype(F32)[rows_of(n)]
            outs[passed][:, here] = (total[rows_of(1 + passed)] + more).astype(BF16)
            outs[1 - passed][:, here] = total[rows_of(2 - passed)].astype(BF16)


def combine_kernel(weighted_ref, *refs):
    near, others, (out_ref, held_ref, sems) = refs[:3], refs[3:-3], refs[-3:]
    weights = weighted_ref[...]
    high = weights.astype(BF16).astype(F32)
    weights = jnp.concatenate([high, weights - high, high], axis=0).astype(BF16)
    copies = []
    for n, at in enumerate(chunks(out_ref.shape[1])):
        own = sum(piece[:, at].astype(F32) for piece in near)
        rows = jnp.concatenate([own] + [piece[:, at].astype(F32) for piece in others], axis=0)
        high = rows.astype(BF16).astype(F32)
        rows = jnp.concatenate([high, high, rows - high], axis=0).astype(BF16)
        held_ref[:, at] = lax.dot_general(
            weights, rows, (((0,), (0,)), ((), ())), preferred_element_type=F32
        ).astype(BF16)
        copies.append(pltpu.make_async_copy(held_ref.at[:, at], out_ref.at[:, at], sems.at[n]))
        copies[-1].start()
    for copy in copies:
        copy.wait()


def local(states, norm_gain, w_gate, w_up, w_down, expert_ids, gate_weights):
    tokens, width = states.shape
    hid = w_gate.shape[1]
    devices = lax.axis_size("tp")
    waves = devices // SPLIT
    others = range(1, waves)

    def swap(x, mask):
        return lax.ppermute(x, "tp", [(i, i ^ mask) for i in range(devices)])

    def cross(x, j):
        return swap(x, SPLIT * j + 4)

    def shape(rows, columns, dtype=BF16):
        return jax.ShapeDtypeStruct((rows, columns), dtype)

    block = shape(CAP, width)

    def stack(pieces):
        rows = sum(x.shape[0] for x in pieces)
        return call(stack_kernel, shape(rows, width), pieces, moved=4 * rows * width)

    gain = norm_gain[None, :]
    ids, gates = expert_ids.T, gate_weights.T
    own, *away, weighted = call(
        functools.partial(pick_kernel, waves),
        [block] * waves + [shape(CAP * waves, tokens, F32)],
        [],
        far_args=[states, gain, ids, gates],
        scratch=[
            pltpu.VMEM((tokens, width), BF16),
            pltpu.VMEM((1, width), F32),
            pltpu.VMEM(ids.shape, ids.dtype),
            pltpu.VMEM(gates.shape, F32),
            pltpu.SemaphoreType.DMA((4,)),
        ],
        flops=2 * tokens * width * CAP * waves,
        moved=tokens * width * 2,
        limit=PICK_LIMIT,
    )
    heads = [cross(away[j - 1], j) for j in others]
    own = call(copy_kernel, block, [own], flops=OWN_FLOPS, moved=4 * CAP * width)

    first = [own] + [swap(own, s) for s in SIDES]
    marks = [call(mark_kernel, shape(CAP, 128, F32), [x]) for x in heads]
    rows = CAP * (waves - 1)
    message = shape(rows, message_width(width, waves - 1))
    far, *sides = call(
        outward_kernel,
        [shape(rows, width), message, message],
        heads + first[1:],
        after=marks,
        moved=12 * rows * width,
    )
    early = stack(first + [far])
    sides = [swap(x, s) for x, s in zip(sides, SIDES)]
    late = call(
        arrived_kernel, shape(3 * rows + CAP, width), sides + [swap(far, CORNER)], moved=16 * rows * width
    )
    blocks = [late, early, swap(late, 1), swap(early, 1)]
    late, early, late_away, early_away = call(
        ffn_kernel,
        [shape(*x.shape) for x in blocks],
        [w_gate, w_up, w_down] + blocks,
        flops=6 * sum(x.shape[0] for x in blocks) * width * hid,
        moved=6 * width * hid,
        limit=24,
    )

    *sides, corner = call(
        homeward_kernel,
        [message, message, shape(rows, width)],
        [late, swap(late_away, 1)],
        moved=20 * rows * width,
    )
    sides = [swap(x, s) for x, s in zip(sides, SIDES)]
    corner = swap(corner, CORNER)
    back = swap(early_away, 1)
    kept = call(
        functools.partial(kept_kernel, CAP * len(first)), shape(rows, width, F32), [early, back], moved=8 * rows * width
    )
    totals = call(total_kernel, [block] * (waves - 1), [kept] + sides + [corner], moved=10 * rows * width)
    returned = [cross(totals[j - 1], j) for j in others]
    kept, *near = call(
        near_kernel, [shape(CAP, width, F32), block, block], [early, back] + sides, after=totals, moved=14 * CAP * width
    )
    near = [kept] + [swap(x, s) for x, s in zip(near, SIDES)]
    marks = [call(mark_kernel, shape(CAP, 128, F32), [x]) for x in returned]
    return call(
        combine_kernel,
        shape(tokens, width),
        [weighted] + near + returned,
        after=marks,
        scratch=[pltpu.VMEM((tokens, width), BF16), pltpu.SemaphoreType.DMA((len(chunks(width)),))],
        out_kind=pl.ANY,
        flops=6 * tokens * width * CAP * waves,
        moved=tokens * width * 4,
    )


def solution(mesh):
    rows = P(("group", "tp"), None)
    in_specs = (rows, P(), P(None, "tp"), P(None, "tp"), P("tp", None), rows, rows)
    return jax.shard_map(local, mesh=mesh, in_specs=in_specs, out_specs=rows, check_vma=False)
```

```python
import functools

import jax
import jax.numpy as jnp
from jax import lax
from jax.experimental import pallas as pl
from jax.experimental.pallas import tpu as pltpu
from jax.sharding import PartitionSpec as P

EXPERTS = 256
NODES = 8
SPLIT = 8
CAP = 8
EPSILON = 1e-06
SIDES = (2, 4)
CORNER = 6
OWN_FLOPS = 7_000_000_000
CHUNK = 1024
F32 = jnp.float32
BF16 = jnp.bfloat16


def call(body, outs, args, after=(), far_args=(), scratch=(), flops=0, moved=0, limit=16, out_kind=pltpu.VMEM):
    left, used = len(far_args), len(far_args) + len(args)

    def run(*refs):
        body(*refs[:used], *refs[used + len(after) :])

    def space(kind):
        return pl.BlockSpec(memory_space=kind)

    far_args = [pltpu.with_memory_space_constraint(x, pltpu.HBM) for x in far_args]
    return pl.pallas_call(
        run,
        out_shape=outs,
        in_specs=[space(pltpu.HBM)] * left + [space(pltpu.VMEM)] * len(args) + [space(pl.ANY)] * len(after),
        out_specs=jax.tree.map(lambda _: space(out_kind), outs),
        scratch_shapes=list(scratch),
        compiler_params=pltpu.CompilerParams(vmem_limit_bytes=limit * 1024 * 1024),
        cost_estimate=pl.CostEstimate(flops=flops, bytes_accessed=moved, transcendentals=0),
    )(*far_args, *args, *after)


def chunks(width):
    return [slice(at, min(at + CHUNK, width)) for at in range(0, width, CHUNK)]


def normed(picked, states_ref, gain_ref):
    rows = jnp.dot(picked, states_ref[...], preferred_element_type=F32)
    squares = jnp.mean(rows * rows, axis=1, keepdims=True)
    return rows * lax.rsqrt(squares + EPSILON) * gain_ref[...]


def pick_kernel(waves, states_hbm, gain_hbm, ids_hbm, gates_hbm, *refs):
    row_refs, weighted_ref = refs[:waves], refs[waves]
    states_ref, gain_ref, ids_ref, gates_ref, sems = refs[waves + 1 :]
    copies = [
        pltpu.make_async_copy(source, target, sems.at[n])
        for n, (source, target) in enumerate(
            [(ids_hbm, ids_ref), (states_hbm, states_ref), (gates_hbm, gates_ref), (gain_hbm, gain_ref)]
        )
    ]
    for copy in copies:
        copy.start()
    tokens = ids_ref.shape[1]
    own = lax.axis_index("tp") // SPLIT
    upper = lax.broadcasted_iota(jnp.int32, (tokens, tokens), 0)
    upper = (upper <= lax.broadcasted_iota(jnp.int32, (tokens, tokens), 1)).astype(F32).astype(BF16)
    slot = lax.broadcasted_iota(jnp.int32, (CAP, tokens), 0).astype(F32)
    copies[0].wait()
    picks = []
    for j in range(waves):
        target = lax.bitwise_xor(own, j) * (EXPERTS // NODES)
        matched = ids_ref[...] == target
        hit = jnp.sum(jnp.where(matched, 1.0, 0.0), axis=0, keepdims=True)
        hits = jnp.broadcast_to(hit, (CAP, tokens))
        place = jnp.dot(hits.astype(BF16), upper, preferred_element_type=F32) - 1.0
        picks.append(jnp.where((hits > 0.5) & (place == slot), 1.0, 0.0))
    for copy in copies[1:]:
        copy.wait()
    for j, picked in enumerate(picks):
        matched = ids_ref[...] == lax.bitwise_xor(own, j) * (EXPERTS // NODES)
        score = jnp.sum(jnp.where(matched, gates_ref[...], 0.0), axis=0, keepdims=True)
        weighted_ref[CAP * j : CAP * (j + 1), :] = picked * score
    rows = normed(jnp.concatenate(picks, axis=0).astype(BF16), states_ref, gain_ref)
    for j, ref in enumerate(row_refs):
        ref[...] = rows[CAP * j : CAP * (j + 1)].astype(BF16)


def ready_kernel(ref, weighted_ref, out_ref, weights_ref):
    out_ref[...] = ref[...]
    weights = weighted_ref[...]
    high = weights.astype(BF16).astype(F32)
    weights_ref[...] = jnp.concatenate([high, weights - high, high], axis=0).T.astype(BF16)


def stack_kernel(*refs):
    for at in chunks(refs[-1].shape[1]):
        parts = [ref[:, at].astype(F32) for ref in refs[:-1]]
        refs[-1][:, at] = jnp.concatenate(parts, axis=0).astype(BF16)


def mark_kernel(ref, out_ref):
    out_ref[...] = ref[:, :128].astype(F32)


def ffn_kernel(gate_ref, up_ref, down_ref, *refs):
    blocks, outs = refs[: len(refs) // 2], refs[len(refs) // 2 :]
    width = blocks[0].shape[1]
    gated = up = 0.0
    for at in chunks(width):
        both = jnp.concatenate([block[:, at].astype(F32) for block in blocks], axis=0).astype(BF16)
        gated += jnp.dot(both, gate_ref[at, :], preferred_element_type=F32)
        up += jnp.dot(both, up_ref[at, :], preferred_element_type=F32)
    hidden = (gated / (1.0 + jnp.exp(-gated)) * up).astype(BF16)
    for at in chunks(width):
        result = jnp.dot(hidden, down_ref[:, at], preferred_element_type=F32)
        first = 0
        for out in outs:
            out[:, at] = result[first : first + out.shape[0]].astype(BF16)
            first += out.shape[0]


def halves(width):
    middle = width // 256 * 128
    return slice(0, middle), slice(middle, width)


def extras(width, blocks, half):
    size = half.stop - half.start
    per = -(-size // (128 * blocks)) * 128
    spans = [(at, min(at + per, size)) for at in range(0, size, per)]
    return [(n, slice(width, width + b - a), slice(half.start + a, half.start + b)) for n, (a, b) in enumerate(spans)]


def message_width(width, blocks):
    return width + max(-(-(h.stop - h.start) // (128 * blocks)) * 128 for h in halves(width))


def rows_of(n):
    return slice(CAP * n, CAP * (n + 1))


def homeward_kernel(home_ref, back_ref, *outs):
    sides, corner = outs[:2], outs[2]
    rows, width = corner.shape
    blocks = rows // CAP
    left, right = halves(width)
    for side, half in zip(sides, (right, left)):
        for n, there, here in extras(width, blocks, half):
            for at in chunks(here.stop - here.start):
                at_here = slice(here.start + at.start, here.start + at.stop)
                at_there = slice(there.start + at.start, there.start + at.stop)
                total = home_ref[:, at_here].astype(F32) + back_ref[:, at_here].astype(F32)
                for k, out in enumerate(outs):
                    out[:, at_here] = total[rows * k : rows * (k + 1)].astype(BF16)
                mine = total[3 * rows :]
                if blocks == 1:
                    side[:, at_there] = mine.astype(BF16)
                else:
                    before = side[:, at_there].astype(F32)
                    pieces = [mine if b == n else before[rows_of(b)] for b in range(blocks)]
                    side[:, at_there] = jnp.concatenate(pieces, axis=0).astype(BF16)


def kept_kernel(skip, home_ref, back_ref, out_ref):
    for at in chunks(home_ref.shape[1]):
        total = home_ref[:, at].astype(F32) + back_ref[:, at].astype(F32)
        out_ref[:, at] = total[skip:]


def total_kernel(*refs):
    arrays, outs = refs[:4], refs[4:]
    for at in chunks(arrays[0].shape[1]):
        total = sum(ref[:, at].astype(F32) for ref in arrays)
        for n, out in enumerate(outs):
            out[:, at] = total[rows_of(n)].astype(BF16)


def near_kernel(home_ref, back_ref, side_one, side_two, kept_ref, one_ref, two_ref):
    width = home_ref.shape[1]
    blocks = side_one.shape[0] // CAP
    left, right = halves(width)
    outs = (one_ref, two_ref)
    for side, half, passed in ((side_two, left, 0), (side_one, right, 1)):
        for n, there, here in extras(width, blocks, half):
            total = home_ref[:, here].astype(F32) + back_ref[:, here].astype(F32)
            kept_ref[:, here] = total[rows_of(0)]
            more = side[:, there].astype(F32)[rows_of(n)]
            outs[passed][:, here] = (total[rows_of(1 + passed)] + more).astype(BF16)
            outs[1 - passed][:, here] = total[rows_of(2 - passed)].astype(BF16)


def combine_kernel(weights_ref, *refs):
    near, others, (out_ref, held_ref, sems) = refs[:3], refs[3:-3], refs[-3:]
    weights = weights_ref[...]
    copies = []
    for n, at in enumerate(chunks(out_ref.shape[1])):
        own = sum(piece[:, at].astype(F32) for piece in near)
        rows = jnp.concatenate([own] + [piece[:, at].astype(F32) for piece in others], axis=0)
        high = rows.astype(BF16).astype(F32)
        rows = jnp.concatenate([high, high, rows - high], axis=0).astype(BF16)
        held_ref[:, at] = jnp.dot(weights, rows, preferred_element_type=F32).astype(BF16)
        copies.append(pltpu.make_async_copy(held_ref.at[:, at], out_ref.at[:, at], sems.at[n]))
        copies[-1].start()
    for copy in copies:
        copy.wait()


def local(states, norm_gain, w_gate, w_up, w_down, expert_ids, gate_weights):
    tokens, width = states.shape
    hid = w_gate.shape[1]
    devices = lax.axis_size("tp")
    waves = devices // SPLIT
    others = range(1, waves)

    def swap(x, mask):
        return lax.ppermute(x, "tp", [(i, i ^ mask) for i in range(devices)])

    def cross(x, j):
        return swap(x, SPLIT * j + 4)

    def shape(rows, columns, dtype=BF16):
        return jax.ShapeDtypeStruct((rows, columns), dtype)

    block = shape(CAP, width)

    def stack(pieces, after=()):
        rows = sum(x.shape[0] for x in pieces)
        return call(stack_kernel, shape(rows, width), pieces, after, moved=4 * rows * width)

    gain = norm_gain[None, :]
    ids, gates = expert_ids.T, gate_weights.T
    own, *away, weighted = call(
        functools.partial(pick_kernel, waves),
        [block] * waves + [shape(CAP * waves, tokens, F32)],
        [],
        far_args=[states, gain, ids, gates],
        scratch=[
            pltpu.VMEM((tokens, width), BF16),
            pltpu.VMEM((1, width), F32),
            pltpu.VMEM(ids.shape, ids.dtype),
            pltpu.VMEM(gates.shape, F32),
            pltpu.SemaphoreType.DMA((4,)),
        ],
        flops=2 * tokens * width * CAP * waves,
        moved=tokens * width * 2,
    )
    side_two = swap(own, SIDES[1])
    heads = [cross(away[j - 1], j) for j in others]
    own, weights = call(
        ready_kernel,
        [block, shape(tokens, 3 * CAP * waves)],
        [own, weighted],
        flops=OWN_FLOPS,
        moved=4 * CAP * width,
    )

    first = [own, swap(own, SIDES[0]), side_two]
    past = swap(first[2], SIDES[0])
    rows = CAP * (waves - 1)
    message = shape(rows, message_width(width, waves - 1))
    far = heads[0] if waves == 2 else stack(heads)
    sent = [swap(far, s) for s in SIDES + (CORNER,)]
    marks = [call(mark_kernel, shape(CAP, 128, F32), [x]) for x in heads]
    early = stack(first + [far], after=marks)
    late = stack(sent + [past])
    blocks = [late, early, swap(late, 1), swap(early, 1)]
    late, early, late_away, early_away = call(
        ffn_kernel,
        [shape(*x.shape) for x in blocks],
        [w_gate, w_up, w_down] + blocks,
        flops=6 * sum(x.shape[0] for x in blocks) * width * hid,
        moved=6 * width * hid,
        limit=24,
    )

    *sides, corner = call(
        homeward_kernel,
        [message, message, shape(rows, width)],
        [late, swap(late_away, 1)],
        moved=20 * rows * width,
    )
    sides = [swap(x, s) for x, s in zip(sides, SIDES)]
    corner = swap(corner, CORNER)
    back = swap(early_away, 1)
    kept = call(
        functools.partial(kept_kernel, CAP * len(first)), shape(rows, width, F32), [early, back], moved=8 * rows * width
    )
    totals = call(total_kernel, [block] * (waves - 1), [kept] + sides + [corner], moved=10 * rows * width)
    returned = [cross(totals[j - 1], j) for j in others]
    kept, *near = call(
        near_kernel, [shape(CAP, width, F32), block, block], [early, back] + sides, after=totals, moved=14 * CAP * width
    )
    near = [kept] + [swap(x, s) for x, s in zip(near, SIDES)]
    marks = [call(mark_kernel, shape(CAP, 128, F32), [x]) for x in returned]
    return call(
        combine_kernel,
        shape(tokens, width),
        [weights] + near + returned,
        after=marks,
        scratch=[pltpu.VMEM((tokens, width), BF16), pltpu.SemaphoreType.DMA((len(chunks(width)),))],
        out_kind=pl.ANY,
        flops=6 * tokens * width * CAP * waves,
        moved=tokens * width * 4,
    )


def solution(mesh):
    rows = P(("group", "tp"), None)
    in_specs = (rows, P(), P(None, "tp"), P(None, "tp"), P("tp", None), rows, rows)
    return jax.shard_map(local, mesh=mesh, in_specs=in_specs, out_specs=rows, check_vma=False)
```

```python
import functools

import jax
import jax.numpy as jnp
from jax import lax
from jax.experimental import pallas as pl
from jax.experimental.pallas import tpu as pltpu
from jax.sharding import PartitionSpec as P

EXPERTS = 256
NODES = 8
SPLIT = 8
CAP = 8
EPSILON = 1e-06
SIDES = (2, 4)
CORNER = 6
OWN_FLOPS = 7_000_000_000
CHUNK = 1024
F32 = jnp.float32
BF16 = jnp.bfloat16


def call(body, outs, args, after=(), far_args=(), scratch=(), flops=0, moved=0, limit=16, out_kind=pltpu.VMEM):
    left, used = len(far_args), len(far_args) + len(args)

    def run(*refs):
        body(*refs[:used], *refs[used + len(after) :])

    def space(kind):
        return pl.BlockSpec(memory_space=kind)

    far_args = [pltpu.with_memory_space_constraint(x, pltpu.HBM) for x in far_args]
    return pl.pallas_call(
        run,
        out_shape=outs,
        in_specs=[space(pltpu.HBM)] * left + [space(pltpu.VMEM)] * len(args) + [space(pl.ANY)] * len(after),
        out_specs=jax.tree.map(lambda _: space(out_kind), outs),
        scratch_shapes=list(scratch),
        compiler_params=pltpu.CompilerParams(vmem_limit_bytes=limit * 1024 * 1024),
        cost_estimate=pl.CostEstimate(flops=flops, bytes_accessed=moved, transcendentals=0),
    )(*far_args, *args, *after)


def chunks(width):
    return [slice(at, min(at + CHUNK, width)) for at in range(0, width, CHUNK)]


def normed(picked, states_ref, gain_ref):
    rows = jnp.dot(picked, states_ref[...], preferred_element_type=F32)
    squares = jnp.mean(rows * rows, axis=1, keepdims=True)
    return rows * lax.rsqrt(squares + EPSILON) * gain_ref[...]


def pick_kernel(waves, states_hbm, gain_hbm, ids_hbm, gates_hbm, *refs):
    row_refs, weighted_ref = refs[:waves], refs[waves]
    states_ref, gain_ref, ids_ref, gates_ref, sems = refs[waves + 1 :]
    copies = [
        pltpu.make_async_copy(source, target, sems.at[n])
        for n, (source, target) in enumerate(
            [(ids_hbm, ids_ref), (states_hbm, states_ref), (gates_hbm, gates_ref), (gain_hbm, gain_ref)]
        )
    ]
    for copy in copies:
        copy.start()
    tokens = ids_ref.shape[1]
    own = lax.axis_index("tp") // SPLIT
    upper = lax.broadcasted_iota(jnp.int32, (tokens, tokens), 0)
    upper = (upper <= lax.broadcasted_iota(jnp.int32, (tokens, tokens), 1)).astype(F32).astype(BF16)
    slot = lax.broadcasted_iota(jnp.int32, (CAP, tokens), 0).astype(F32)
    copies[0].wait()
    picks = []
    for j in range(waves):
        target = lax.bitwise_xor(own, j) * (EXPERTS // NODES)
        matched = ids_ref[...] == target
        hit = jnp.sum(jnp.where(matched, 1.0, 0.0), axis=0, keepdims=True)
        hits = jnp.broadcast_to(hit, (CAP, tokens))
        place = jnp.dot(hits.astype(BF16), upper, preferred_element_type=F32) - 1.0
        picks.append(jnp.where((hits > 0.5) & (place == slot), 1.0, 0.0))
    for copy in copies[1:]:
        copy.wait()
    for j, picked in enumerate(picks):
        matched = ids_ref[...] == lax.bitwise_xor(own, j) * (EXPERTS // NODES)
        score = jnp.sum(jnp.where(matched, gates_ref[...], 0.0), axis=0, keepdims=True)
        weighted_ref[CAP * j : CAP * (j + 1), :] = picked * score
    rows = normed(jnp.concatenate(picks, axis=0).astype(BF16), states_ref, gain_ref)
    for j, ref in enumerate(row_refs):
        ref[...] = rows[CAP * j : CAP * (j + 1)].astype(BF16)


def ready_kernel(ref, weighted_ref, out_ref, weights_ref):
    out_ref[...] = ref[...]
    weights = weighted_ref[...]
    high = weights.astype(BF16).astype(F32)
    weights_ref[...] = jnp.concatenate([high, weights - high, high], axis=0).T.astype(BF16)


def stack_kernel(*refs):
    for at in chunks(refs[-1].shape[1]):
        parts = [ref[:, at].astype(F32) for ref in refs[:-1]]
        refs[-1][:, at] = jnp.concatenate(parts, axis=0).astype(BF16)


def mark_kernel(ref, out_ref):
    out_ref[...] = ref[:, :128].astype(F32)


def ffn_kernel(gate_ref, up_ref, down_ref, *refs):
    blocks, outs = refs[: len(refs) // 2], refs[len(refs) // 2 :]
    width = blocks[0].shape[1]
    gated = up = 0.0
    for at in chunks(width):
        both = jnp.concatenate([block[:, at].astype(F32) for block in blocks], axis=0).astype(BF16)
        gated += jnp.dot(both, gate_ref[at, :], preferred_element_type=F32)
        up += jnp.dot(both, up_ref[at, :], preferred_element_type=F32)
    hidden = (gated / (1.0 + jnp.exp(-gated)) * up).astype(BF16)
    for at in chunks(width):
        result = jnp.dot(hidden, down_ref[:, at], preferred_element_type=F32)
        first = 0
        for out in outs:
            out[:, at] = result[first : first + out.shape[0]].astype(BF16)
            first += out.shape[0]


def rows_of(n):
    return slice(CAP * n, CAP * (n + 1))


def pair_kernel(first, home_ref, back_ref, *outs):
    for at in chunks(home_ref.shape[1]):
        total = home_ref[:, at].astype(F32) + back_ref[:, at].astype(F32)
        row = first
        for out in outs:
            out[:, at] = total[row : row + out.shape[0]].astype(out.dtype)
            row += out.shape[0]


def passed_kernel(first, home_ref, back_ref, more_ref, out_ref):
    for at in chunks(home_ref.shape[1]):
        total = home_ref[:, at].astype(F32) + back_ref[:, at].astype(F32)
        out_ref[:, at] = (total[first : first + CAP] + more_ref[:, at].astype(F32)).astype(BF16)


def total_kernel(*refs):
    arrays, outs = refs[:4], refs[4:]
    for at in chunks(arrays[0].shape[1]):
        total = sum(ref[:, at].astype(F32) for ref in arrays)
        for n, out in enumerate(outs):
            out[:, at] = total[rows_of(n)].astype(BF16)


def combine_kernel(weights_ref, *refs):
    near, others, (out_ref, held_ref, sems) = refs[:3], refs[3:-3], refs[-3:]
    weights = weights_ref[...]
    copies = []
    for n, at in enumerate(chunks(out_ref.shape[1])):
        own = sum(piece[:, at].astype(F32) for piece in near)
        rows = jnp.concatenate([own] + [piece[:, at].astype(F32) for piece in others], axis=0)
        high = rows.astype(BF16).astype(F32)
        rows = jnp.concatenate([high, high, rows - high], axis=0).astype(BF16)
        held_ref[:, at] = jnp.dot(weights, rows, preferred_element_type=F32).astype(BF16)
        copies.append(pltpu.make_async_copy(held_ref.at[:, at], out_ref.at[:, at], sems.at[n]))
        copies[-1].start()
    for copy in copies:
        copy.wait()


def local(states, norm_gain, w_gate, w_up, w_down, expert_ids, gate_weights):
    tokens, width = states.shape
    hid = w_gate.shape[1]
    devices = lax.axis_size("tp")
    waves = devices // SPLIT
    others = range(1, waves)

    def swap(x, mask):
        return lax.ppermute(x, "tp", [(i, i ^ mask) for i in range(devices)])

    def cross(x, j):
        return swap(x, SPLIT * j + 4)

    def shape(rows, columns, dtype=BF16):
        return jax.ShapeDtypeStruct((rows, columns), dtype)

    block = shape(CAP, width)

    def stack(pieces, after=()):
        rows = sum(x.shape[0] for x in pieces)
        return call(stack_kernel, shape(rows, width), pieces, after, moved=4 * rows * width)

    gain = norm_gain[None, :]
    ids, gates = expert_ids.T, gate_weights.T
    own, *away, weighted = call(
        functools.partial(pick_kernel, waves),
        [block] * waves + [shape(CAP * waves, tokens, F32)],
        [],
        far_args=[states, gain, ids, gates],
        scratch=[
            pltpu.VMEM((tokens, width), BF16),
            pltpu.VMEM((1, width), F32),
            pltpu.VMEM(ids.shape, ids.dtype),
            pltpu.VMEM(gates.shape, F32),
            pltpu.SemaphoreType.DMA((4,)),
        ],
        flops=2 * tokens * width * CAP * waves,
        moved=tokens * width * 2,
    )
    side_two = swap(own, SIDES[1])
    heads = [cross(away[j - 1], j) for j in others]
    own, weights = call(
        ready_kernel,
        [block, shape(tokens, 3 * CAP * waves)],
        [own, weighted],
        flops=OWN_FLOPS,
        moved=4 * CAP * width,
    )

    first = [own, swap(own, SIDES[0]), side_two]
    past = swap(first[2], SIDES[0])
    rows = CAP * (waves - 1)
    far = heads[0] if waves == 2 else stack(heads)
    sent = [swap(far, s) for s in SIDES + (CORNER,)]
    marks = [call(mark_kernel, shape(CAP, 128, F32), [x]) for x in heads]
    early = stack(first + [far], after=marks)
    late = stack(sent + [past])
    blocks = [late, early, swap(late, 1), swap(early, 1)]
    late, early, late_away, early_away = call(
        ffn_kernel,
        [shape(*x.shape) for x in blocks],
        [w_gate, w_up, w_down] + blocks,
        flops=6 * sum(x.shape[0] for x in blocks) * width * hid,
        moved=6 * width * hid,
        limit=24,
    )

    def pair(home, back, first, outs, after=()):
        body = functools.partial(pair_kernel, CAP * first)
        moved = sum(6 * out.shape[0] * width for out in outs)
        return call(body, outs, [home, back], after, moved=moved)

    *sent, past = pair(late, swap(late_away, 1), 0, [shape(rows, width)] * 3 + [block])
    sent = [swap(x, s) for x, s in zip(sent, SIDES + (CORNER,))]
    past = swap(past, SIDES[0])
    back = swap(early_away, 1)
    (kept,) = pair(early, back, len(first), [shape(rows, width, F32)])
    totals = call(total_kernel, [block] * (waves - 1), [kept] + sent, moved=10 * rows * width)
    returned = [cross(totals[j - 1], j) for j in others]
    kept, one = pair(early, back, 0, [shape(CAP, width, F32), block], after=totals)
    body = functools.partial(passed_kernel, 2 * CAP)
    two = call(body, block, [early, back, past], after=[one], moved=10 * CAP * width)
    near = [kept, swap(one, SIDES[0]), swap(two, SIDES[1])]
    marks = [call(mark_kernel, shape(CAP, 128, F32), [x]) for x in returned]
    return call(
        combine_kernel,
        shape(tokens, width),
        [weights] + near + returned,
        after=marks,
        scratch=[pltpu.VMEM((tokens, width), BF16), pltpu.SemaphoreType.DMA((len(chunks(width)),))],
        out_kind=pl.ANY,
        flops=6 * tokens * width * CAP * waves,
        moved=tokens * width * 4,
    )


def solution(mesh):
    rows = P(("group", "tp"), None)
    in_specs = (rows, P(), P(None, "tp"), P(None, "tp"), P("tp", None), rows, rows)
    return jax.shard_map(local, mesh=mesh, in_specs=in_specs, out_specs=rows, check_vma=False)
```

```python
import functools

import jax
import jax.numpy as jnp
from jax import lax
from jax.experimental import pallas as pl
from jax.experimental.pallas import tpu as pltpu
from jax.sharding import PartitionSpec as P

EXPERTS = 256
NODES = 8
SPLIT = 8
CAP = 8
EPSILON = 1e-06
SIDES = (2, 4)
CORNER = 6
OWN_FLOPS = 7_000_000_000
CHUNK = 1024
F32 = jnp.float32
BF16 = jnp.bfloat16


def call(body, outs, args, after=(), far_args=(), scratch=(), flops=0, moved=0, limit=16, out_kind=pltpu.VMEM):
    left, used = len(far_args), len(far_args) + len(args)

    def run(*refs):
        body(*refs[:used], *refs[used + len(after) :])

    def space(kind):
        return pl.BlockSpec(memory_space=kind)

    far_args = [pltpu.with_memory_space_constraint(x, pltpu.HBM) for x in far_args]
    return pl.pallas_call(
        run,
        out_shape=outs,
        in_specs=[space(pltpu.HBM)] * left + [space(pltpu.VMEM)] * len(args) + [space(pl.ANY)] * len(after),
        out_specs=jax.tree.map(lambda _: space(out_kind), outs),
        scratch_shapes=list(scratch),
        compiler_params=pltpu.CompilerParams(vmem_limit_bytes=limit * 1024 * 1024),
        cost_estimate=pl.CostEstimate(flops=flops, bytes_accessed=moved, transcendentals=0),
    )(*far_args, *args, *after)


def chunks(width):
    return [slice(at, min(at + CHUNK, width)) for at in range(0, width, CHUNK)]


def normed(picked, states_ref, gain_ref):
    rows = jnp.dot(picked, states_ref[...], preferred_element_type=F32)
    squares = jnp.mean(rows * rows, axis=1, keepdims=True)
    return rows * lax.rsqrt(squares + EPSILON) * gain_ref[...]


def pick_kernel(waves, states_hbm, gain_hbm, ids_hbm, gates_hbm, *refs):
    row_refs, weighted_ref = refs[:waves], refs[waves]
    states_ref, gain_ref, ids_ref, gates_ref, sems = refs[waves + 1 :]
    copies = [
        pltpu.make_async_copy(source, target, sems.at[n])
        for n, (source, target) in enumerate(
            [(ids_hbm, ids_ref), (states_hbm, states_ref), (gates_hbm, gates_ref), (gain_hbm, gain_ref)]
        )
    ]
    for copy in copies:
        copy.start()
    tokens = ids_ref.shape[1]
    own = lax.axis_index("tp") // SPLIT
    upper = lax.broadcasted_iota(jnp.int32, (tokens, tokens), 0)
    upper = (upper <= lax.broadcasted_iota(jnp.int32, (tokens, tokens), 1)).astype(F32).astype(BF16)
    slot = lax.broadcasted_iota(jnp.int32, (CAP, tokens), 0).astype(F32)
    copies[0].wait()
    picks = []
    for j in range(waves):
        target = lax.bitwise_xor(own, j) * (EXPERTS // NODES)
        matched = ids_ref[...] == target
        hit = jnp.sum(jnp.where(matched, 1.0, 0.0), axis=0, keepdims=True)
        hits = jnp.broadcast_to(hit, (CAP, tokens))
        place = jnp.dot(hits.astype(BF16), upper, preferred_element_type=F32) - 1.0
        picks.append(jnp.where((hits > 0.5) & (place == slot), 1.0, 0.0))
    for copy in copies[1:]:
        copy.wait()
    for j, picked in enumerate(picks):
        matched = ids_ref[...] == lax.bitwise_xor(own, j) * (EXPERTS // NODES)
        score = jnp.sum(jnp.where(matched, gates_ref[...], 0.0), axis=0, keepdims=True)
        weighted_ref[CAP * j : CAP * (j + 1), :] = picked * score
    rows = normed(jnp.concatenate(picks, axis=0).astype(BF16), states_ref, gain_ref)
    for j, ref in enumerate(row_refs):
        ref[...] = rows[CAP * j : CAP * (j + 1)].astype(BF16)


def ready_kernel(ref, weighted_ref, out_ref, weights_ref):
    out_ref[...] = ref[...]
    weights = weighted_ref[...]
    high = weights.astype(BF16).astype(F32)
    weights_ref[...] = jnp.concatenate([high, weights - high, high], axis=0).T.astype(BF16)


def stack_kernel(*refs):
    for at in chunks(refs[-1].shape[1]):
        parts = [ref[:, at].astype(F32) for ref in refs[:-1]]
        refs[-1][:, at] = jnp.concatenate(parts, axis=0).astype(BF16)


def slice_kernel(start, ref, out_ref):
    out_ref[...] = ref[:, start : start + out_ref.shape[1]]


def late_kernel(*refs):
    *far, left, right, out_ref = refs
    for half, first in ((left, 0), (right, left.shape[1])):
        for at in chunks(half.shape[1]):
            there = slice(first + at.start, first + at.stop)
            parts = [ref[:, there].astype(F32) for ref in far] + [half[:, at].astype(F32)]
            out_ref[:, there] = jnp.concatenate(parts, axis=0).astype(BF16)


def mark_kernel(ref, out_ref):
    out_ref[...] = ref[:, :128].astype(F32)


def ffn_kernel(gate_ref, up_ref, down_ref, *refs):
    blocks, outs = refs[: len(refs) // 2], refs[len(refs) // 2 :]
    width = blocks[0].shape[1]
    gated = up = 0.0
    for at in chunks(width):
        both = jnp.concatenate([block[:, at].astype(F32) for block in blocks], axis=0).astype(BF16)
        gated += jnp.dot(both, gate_ref[at, :], preferred_element_type=F32)
        up += jnp.dot(both, up_ref[at, :], preferred_element_type=F32)
    hidden = (gated / (1.0 + jnp.exp(-gated)) * up).astype(BF16)
    for at in chunks(width):
        result = jnp.dot(hidden, down_ref[:, at], preferred_element_type=F32)
        first = 0
        for out in outs:
            out[:, at] = result[first : first + out.shape[0]].astype(BF16)
            first += out.shape[0]


def rows_of(n):
    return slice(CAP * n, CAP * (n + 1))


def pair_kernel(first, home_ref, back_ref, *outs):
    for at in chunks(home_ref.shape[1]):
        total = home_ref[:, at].astype(F32) + back_ref[:, at].astype(F32)
        row = first
        for out in outs:
            out[:, at] = total[row : row + out.shape[0]].astype(out.dtype)
            row += out.shape[0]


def passed_kernel(first, home_ref, back_ref, more_ref, out_ref):
    for at in chunks(home_ref.shape[1]):
        total = home_ref[:, at].astype(F32) + back_ref[:, at].astype(F32)
        out_ref[:, at] = (total[first : first + CAP] + more_ref[:, at].astype(F32)).astype(BF16)


def total_kernel(*refs):
    arrays, outs = refs[:4], refs[4:]
    for at in chunks(arrays[0].shape[1]):
        total = sum(ref[:, at].astype(F32) for ref in arrays)
        for n, out in enumerate(outs):
            out[:, at] = total[rows_of(n)].astype(BF16)


def combine_kernel(weights_ref, *refs):
    near, others, (out_ref, held_ref, sems) = refs[:3], refs[3:-3], refs[-3:]
    weights = weights_ref[...]
    copies = []
    for n, at in enumerate(chunks(out_ref.shape[1])):
        own = sum(piece[:, at].astype(F32) for piece in near)
        rows = jnp.concatenate([own] + [piece[:, at].astype(F32) for piece in others], axis=0)
        high = rows.astype(BF16).astype(F32)
        rows = jnp.concatenate([high, high, rows - high], axis=0).astype(BF16)
        held_ref[:, at] = jnp.dot(weights, rows, preferred_element_type=F32).astype(BF16)
        copies.append(pltpu.make_async_copy(held_ref.at[:, at], out_ref.at[:, at], sems.at[n]))
        copies[-1].start()
    for copy in copies:
        copy.wait()


def local(states, norm_gain, w_gate, w_up, w_down, expert_ids, gate_weights):
    tokens, width = states.shape
    hid = w_gate.shape[1]
    devices = lax.axis_size("tp")
    waves = devices // SPLIT
    others = range(1, waves)

    def swap(x, mask):
        return lax.ppermute(x, "tp", [(i, i ^ mask) for i in range(devices)])

    def cross(x, j):
        return swap(x, SPLIT * j + 4)

    def shape(rows, columns, dtype=BF16):
        return jax.ShapeDtypeStruct((rows, columns), dtype)

    block = shape(CAP, width)

    def stack(pieces, after=()):
        rows = sum(x.shape[0] for x in pieces)
        return call(stack_kernel, shape(rows, width), pieces, after, moved=4 * rows * width)

    gain = norm_gain[None, :]
    ids, gates = expert_ids.T, gate_weights.T
    own, *away, weighted = call(
        functools.partial(pick_kernel, waves),
        [block] * waves + [shape(CAP * waves, tokens, F32)],
        [],
        far_args=[states, gain, ids, gates],
        scratch=[
            pltpu.VMEM((tokens, width), BF16),
            pltpu.VMEM((1, width), F32),
            pltpu.VMEM(ids.shape, ids.dtype),
            pltpu.VMEM(gates.shape, F32),
            pltpu.SemaphoreType.DMA((4,)),
        ],
        flops=2 * tokens * width * CAP * waves,
        moved=tokens * width * 2,
    )
    side_two = swap(own, SIDES[1])
    heads = [cross(away[j - 1], j) for j in others]
    own, weights = call(
        ready_kernel,
        [block, shape(tokens, 3 * CAP * waves)],
        [own, weighted],
        flops=OWN_FLOPS,
        moved=4 * CAP * width,
    )

    first = [own, swap(own, SIDES[0]), side_two]
    middle = width // 256 * 128
    left = call(functools.partial(slice_kernel, 0), shape(CAP, middle), [first[1]], moved=4 * CAP * middle)
    right = call(
        functools.partial(slice_kernel, middle), shape(CAP, width - middle), [first[2]], moved=4 * CAP * middle
    )
    past = [swap(left, SIDES[1]), swap(right, SIDES[0])]
    rows = CAP * (waves - 1)
    far = heads[0] if waves == 2 else stack(heads)
    sent = [swap(far, s) for s in SIDES + (CORNER,)]
    marks = [call(mark_kernel, shape(CAP, 128, F32), [x]) for x in heads]
    early = stack(first + [far], after=marks)
    late = call(late_kernel, shape(3 * rows + CAP, width), sent + past, moved=16 * rows * width)
    blocks = [late, early, swap(late, 1), swap(early, 1)]
    late, early, late_away, early_away = call(
        ffn_kernel,
        [shape(*x.shape) for x in blocks],
        [w_gate, w_up, w_down] + blocks,
        flops=6 * sum(x.shape[0] for x in blocks) * width * hid,
        moved=6 * width * hid,
        limit=24,
    )

    def pair(home, back, first, outs, after=()):
        body = functools.partial(pair_kernel, CAP * first)
        moved = sum(6 * out.shape[0] * width for out in outs)
        return call(body, outs, [home, back], after, moved=moved)

    *sent, past = pair(late, swap(late_away, 1), 0, [shape(rows, width)] * 3 + [block])
    sent = [swap(x, s) for x, s in zip(sent, SIDES + (CORNER,))]
    past = swap(past, SIDES[0])
    back = swap(early_away, 1)
    (kept,) = pair(early, back, len(first), [shape(rows, width, F32)])
    totals = call(total_kernel, [block] * (waves - 1), [kept] + sent, moved=10 * rows * width)
    returned = [cross(totals[j - 1], j) for j in others]
    kept, one = pair(early, back, 0, [shape(CAP, width, F32), block], after=totals)
    body = functools.partial(passed_kernel, 2 * CAP)
    two = call(body, block, [early, back, past], after=[one], moved=10 * CAP * width)
    near = [kept, swap(one, SIDES[0]), swap(two, SIDES[1])]
    marks = [call(mark_kernel, shape(CAP, 128, F32), [x]) for x in returned]
    return call(
        combine_kernel,
        shape(tokens, width),
        [weights] + near + returned,
        after=marks,
        scratch=[pltpu.VMEM((tokens, width), BF16), pltpu.SemaphoreType.DMA((len(chunks(width)),))],
        out_kind=pl.ANY,
        flops=6 * tokens * width * CAP * waves,
        moved=tokens * width * 4,
    )


def solution(mesh):
    rows = P(("group", "tp"), None)
    in_specs = (rows, P(), P(None, "tp"), P(None, "tp"), P("tp", None), rows, rows)
    return jax.shard_map(local, mesh=mesh, in_specs=in_specs, out_specs=rows, check_vma=False)
```

```python
import functools

import jax
import jax.numpy as jnp
from jax import lax
from jax.experimental import pallas as pl
from jax.experimental.pallas import tpu as pltpu
from jax.sharding import PartitionSpec as P

EXPERTS = 256
NODES = 8
SPLIT = 8
CAP = 8
EPSILON = 1e-06
SIDES = ((2, 2), (4, 4))
MIXED = ((2, 4), (4, 2))
CORNER = (6, 6)
OTHER = (1, 1)
OWN_FLOPS = 7_000_000_000
CHUNK = 1024
OUT_CHUNK = 1792
F32 = jnp.float32
BF16 = jnp.bfloat16


def call(body, outs, args, after=(), far_args=(), scratch=(), flops=0, moved=0, limit=16, out_kind=pltpu.VMEM):
    left, used = len(far_args), len(far_args) + len(args)

    def run(*refs):
        body(*refs[:used], *refs[used + len(after) :])

    def space(kind):
        return pl.BlockSpec(memory_space=kind)

    far_args = [pltpu.with_memory_space_constraint(x, pltpu.HBM) for x in far_args]
    return pl.pallas_call(
        run,
        out_shape=outs,
        in_specs=[space(pltpu.HBM)] * left + [space(pltpu.VMEM)] * len(args) + [space(pl.ANY)] * len(after),
        out_specs=jax.tree.map(lambda _: space(out_kind), outs),
        scratch_shapes=list(scratch),
        compiler_params=pltpu.CompilerParams(vmem_limit_bytes=limit * 1024 * 1024),
        cost_estimate=pl.CostEstimate(flops=flops, bytes_accessed=moved, transcendentals=0),
    )(*far_args, *args, *after)


def chunks(width, size=CHUNK):
    return [slice(at, min(at + size, width)) for at in range(0, width, size)]


def pick_kernel(waves, states_hbm, gain_hbm, ids_hbm, gates_hbm, *refs):
    row_refs, weighted_ref = refs[:waves], refs[waves]
    states_ref, rows_ref, gain_ref, ids_ref, gates_ref, sems = refs[waves + 1 :]
    copies = [
        pltpu.make_async_copy(source, target, sems.at[n])
        for n, (source, target) in enumerate(
            [(ids_hbm, ids_ref), (states_hbm, states_ref), (gates_hbm, gates_ref), (gain_hbm, gain_ref)]
        )
    ]
    for copy in copies:
        copy.start()
    tokens = ids_ref.shape[1]
    own = lax.axis_index("tp") // SPLIT
    upper = lax.broadcasted_iota(jnp.int32, (tokens, tokens), 0)
    upper = (upper <= lax.broadcasted_iota(jnp.int32, (tokens, tokens), 1)).astype(F32).astype(BF16)
    slot = lax.broadcasted_iota(jnp.int32, (CAP, tokens), 0).astype(F32)
    copies[0].wait()
    picks = []
    for j in range(waves):
        target = lax.bitwise_xor(own, j) * (EXPERTS // NODES)
        matched = ids_ref[...] == target
        hit = jnp.sum(jnp.where(matched, 1.0, 0.0), axis=0, keepdims=True)
        hits = jnp.broadcast_to(hit, (CAP, tokens))
        place = jnp.dot(hits.astype(BF16), upper, preferred_element_type=F32) - 1.0
        picks.append(jnp.where((hits > 0.5) & (place == slot), 1.0, 0.0))
    for copy in copies[1:]:
        copy.wait()
    for j, picked in enumerate(picks):
        matched = ids_ref[...] == lax.bitwise_xor(own, j) * (EXPERTS // NODES)
        score = jnp.sum(jnp.where(matched, gates_ref[...], 0.0), axis=0, keepdims=True)
        weighted_ref[CAP * j : CAP * (j + 1), :] = picked * score
    picked = jnp.concatenate(picks, axis=0).astype(BF16)
    width = states_ref.shape[1]
    squares = 0.0
    for at in chunks(width):
        rows = jnp.dot(picked, states_ref[:, at], preferred_element_type=F32)
        rows_ref[:, at] = rows
        squares += jnp.sum(rows * rows, axis=1, keepdims=True)
    scale = lax.rsqrt(squares / width + EPSILON)
    for at in chunks(width):
        rows = rows_ref[:, at] * scale * gain_ref[:, at]
        for j, ref in enumerate(row_refs):
            ref[:, at] = rows[CAP * j : CAP * (j + 1)].astype(BF16)


def ready_kernel(ref, weighted_ref, out_ref, weights_ref):
    out_ref[...] = ref[...]
    weights = weighted_ref[...]
    high = weights.astype(BF16).astype(F32)
    weights_ref[...] = jnp.concatenate([high, weights - high, high], axis=0).T.astype(BF16)


def stack_kernel(*refs):
    for at in chunks(refs[-1].shape[1]):
        parts = [ref[:, at].astype(F32) for ref in refs[:-1]]
        refs[-1][:, at] = jnp.concatenate(parts, axis=0).astype(BF16)


def choose_kernel(even_ref, odd_ref, out_ref):
    even = lax.axis_index("tp") % 2 == 0

    @pl.when(even)
    def _():
        out_ref[...] = even_ref[...]

    @pl.when(jnp.logical_not(even))
    def _():
        out_ref[...] = odd_ref[...]


def mark_kernel(ref, out_ref):
    out_ref[...] = ref[:, :128].astype(F32)


def ffn_kernel(gate_ref, up_ref, down_ref, *refs):
    blocks, outs = refs[: len(refs) // 2], refs[len(refs) // 2 :]
    width = blocks[0].shape[1]
    gated = up = 0.0
    for at in chunks(width):
        both = jnp.concatenate([block[:, at] for block in blocks], axis=0)
        gated += jnp.dot(both, gate_ref[at, :], preferred_element_type=F32)
        up += jnp.dot(both, up_ref[at, :], preferred_element_type=F32)
    hidden = (gated / (1.0 + jnp.exp(-gated)) * up).astype(BF16)
    for at in chunks(width):
        result = jnp.dot(hidden, down_ref[:, at], preferred_element_type=F32)
        first = 0
        for out in outs:
            out[:, at] = result[first : first + out.shape[0]].astype(BF16)
            first += out.shape[0]


def rows_of(n):
    return slice(CAP * n, CAP * (n + 1))


def pair_kernel(first, home_ref, back_ref, *outs):
    for at in chunks(home_ref.shape[1]):
        total = home_ref[:, at].astype(F32) + back_ref[:, at].astype(F32)
        row = first
        for out in outs:
            out[:, at] = total[row : row + out.shape[0]].astype(out.dtype)
            row += out.shape[0]


def passed_kernel(first, home_ref, back_ref, more_ref, out_ref):
    for at in chunks(home_ref.shape[1]):
        total = home_ref[:, at].astype(F32) + back_ref[:, at].astype(F32)
        out_ref[:, at] = (total[first : first + CAP] + more_ref[:, at].astype(F32)).astype(BF16)


def total_kernel(*refs):
    arrays, outs = refs[:4], refs[4:]
    for at in chunks(arrays[0].shape[1]):
        total = sum(ref[:, at].astype(F32) for ref in arrays)
        for n, out in enumerate(outs):
            out[:, at] = total[rows_of(n)].astype(BF16)


def combine_kernel(weights_ref, *refs):
    near, others, (out_ref, held_ref, sems) = refs[:3], refs[3:-3], refs[-3:]
    weights = weights_ref[...]
    copies = []
    for n, at in enumerate(chunks(out_ref.shape[1], OUT_CHUNK)):
        own = sum(piece[:, at].astype(F32) for piece in near)
        rows = jnp.concatenate([own] + [piece[:, at].astype(F32) for piece in others], axis=0)
        high = rows.astype(BF16).astype(F32)
        rows = jnp.concatenate([high, high, rows - high], axis=0).astype(BF16)
        held_ref[:, at] = jnp.dot(weights, rows, preferred_element_type=F32).astype(BF16)
        copies.append(pltpu.make_async_copy(held_ref.at[:, at], out_ref.at[:, at], sems.at[n]))
        copies[-1].start()
    for copy in copies:
        copy.wait()


def local(states, norm_gain, w_gate, w_up, w_down, expert_ids, gate_weights):
    tokens, width = states.shape
    hid = w_gate.shape[1]
    devices = lax.axis_size("tp")
    waves = devices // SPLIT
    others = range(1, waves)

    def swap(x, mask):
        return lax.ppermute(x, "tp", [(i, i ^ mask[i % 2]) for i in range(devices)])

    def cross(x, j):
        return swap(x, (SPLIT * j + 4,) * 2)

    def shape(rows, columns, dtype=BF16):
        return jax.ShapeDtypeStruct((rows, columns), dtype)

    block = shape(CAP, width)

    def stack(pieces, after=()):
        rows = sum(x.shape[0] for x in pieces)
        return call(stack_kernel, shape(rows, width), pieces, after, moved=4 * rows * width)

    gain = norm_gain[None, :]
    ids, gates = expert_ids.T, gate_weights.T
    own, *away, weighted = call(
        functools.partial(pick_kernel, waves),
        [block] * waves + [shape(CAP * waves, tokens, F32)],
        [],
        far_args=[states, gain, ids, gates],
        scratch=[
            pltpu.VMEM((tokens, width), BF16),
            pltpu.VMEM((CAP * waves, width), F32),
            pltpu.VMEM((1, width), F32),
            pltpu.VMEM(ids.shape, ids.dtype),
            pltpu.VMEM(gates.shape, F32),
            pltpu.SemaphoreType.DMA((4,)),
        ],
        flops=2 * tokens * width * CAP * waves,
        moved=tokens * width * 2,
    )
    side_two = swap(own, SIDES[1])
    heads = [cross(away[j - 1], j) for j in others]
    own, weights = call(
        ready_kernel,
        [block, shape(tokens, 3 * CAP * waves)],
        [own, weighted],
        flops=OWN_FLOPS,
        moved=4 * CAP * width,
    )

    first = [own, swap(own, SIDES[0]), side_two]
    past = call(choose_kernel, block, [first[2], first[1]], moved=6 * CAP * width)
    past = swap(past, MIXED[0])
    rows = CAP * (waves - 1)
    far = heads[0] if waves == 2 else stack(heads)
    sent = [swap(far, s) for s in MIXED + (CORNER,)]
    marks = [call(mark_kernel, shape(CAP, 128, F32), [x]) for x in heads]
    early = stack(first + [far], after=marks)
    late = stack(sent + [past])
    blocks = [late, early, swap(late, OTHER), swap(early, OTHER)]
    late, early, late_away, early_away = call(
        ffn_kernel,
        [shape(*x.shape) for x in blocks],
        [w_gate, w_up, w_down] + blocks,
        flops=6 * sum(x.shape[0] for x in blocks) * width * hid,
        moved=6 * width * hid,
        limit=24,
    )

    def pair(home, back, first, outs, after=()):
        body = functools.partial(pair_kernel, CAP * first)
        moved = sum(6 * out.shape[0] * width for out in outs)
        return call(body, outs, [home, back], after, moved=moved)

    *sent, past = pair(late, swap(late_away, OTHER), 0, [shape(rows, width)] * 3 + [block])
    sent = [swap(x, s) for x, s in zip(sent, MIXED + (CORNER,))]
    past = swap(past, SIDES[0])
    back = swap(early_away, OTHER)
    (kept,) = pair(early, back, len(first), [shape(rows, width, F32)])
    totals = call(total_kernel, [block] * (waves - 1), [kept] + sent, moved=10 * rows * width)
    returned = [cross(totals[j - 1], j) for j in others]
    kept, one = pair(early, back, 0, [shape(CAP, width, F32), block], after=totals)
    body = functools.partial(passed_kernel, 2 * CAP)
    two = call(body, block, [early, back, past], after=[one], moved=10 * CAP * width)
    near = [kept, swap(one, SIDES[0]), swap(two, SIDES[1])]
    marks = [call(mark_kernel, shape(CAP, 128, F32), [x]) for x in returned]
    return call(
        combine_kernel,
        shape(tokens, width),
        [weights] + near + returned,
        after=marks,
        scratch=[pltpu.VMEM((tokens, width), BF16), pltpu.SemaphoreType.DMA((len(chunks(width, OUT_CHUNK)),))],
        out_kind=pl.ANY,
        flops=6 * tokens * width * CAP * waves,
        moved=tokens * width * 4,
    )


def solution(mesh):
    rows = P(("group", "tp"), None)
    in_specs = (rows, P(), P(None, "tp"), P(None, "tp"), P("tp", None), rows, rows)
    return jax.shard_map(local, mesh=mesh, in_specs=in_specs, out_specs=rows, check_vma=False)
```

```python
import functools

import jax
import jax.numpy as jnp
from jax import lax
from jax.experimental import pallas as pl
from jax.experimental.pallas import tpu as pltpu
from jax.sharding import PartitionSpec as P

EXPERTS = 256
NODES = 8
SPLIT = 8
CAP = 8
EPSILON = 1e-06
SIDES = ((2, 2), (4, 4))
MIXED = ((4, 2), (2, 4))
CORNER = (6, 6)
OTHER = (1, 1)
OWN_FLOPS = 7_000_000_000
CHUNK = 1024
OUT_CHUNK = 1792
F32 = jnp.float32
BF16 = jnp.bfloat16


def call(body, outs, args, after=(), far_args=(), scratch=(), flops=0, moved=0, limit=16, out_kind=pltpu.VMEM):
    left, used = len(far_args), len(far_args) + len(args)

    def run(*refs):
        body(*refs[:used], *refs[used + len(after) :])

    def space(kind):
        return pl.BlockSpec(memory_space=kind)

    far_args = [pltpu.with_memory_space_constraint(x, pltpu.HBM) for x in far_args]
    return pl.pallas_call(
        run,
        out_shape=outs,
        in_specs=[space(pltpu.HBM)] * left + [space(pltpu.VMEM)] * len(args) + [space(pl.ANY)] * len(after),
        out_specs=jax.tree.map(lambda _: space(out_kind), outs),
        scratch_shapes=list(scratch),
        compiler_params=pltpu.CompilerParams(vmem_limit_bytes=limit * 1024 * 1024),
        cost_estimate=pl.CostEstimate(flops=flops, bytes_accessed=moved, transcendentals=0),
    )(*far_args, *args, *after)


def chunks(width, size=CHUNK):
    return [slice(at, min(at + size, width)) for at in range(0, width, size)]


def pick_kernel(waves, states_hbm, gain_hbm, ids_hbm, gates_hbm, *refs):
    row_refs, weighted_ref = refs[:waves], refs[waves]
    states_ref, rows_ref, gain_ref, ids_ref, gates_ref, sems = refs[waves + 1 :]
    copies = [
        pltpu.make_async_copy(source, target, sems.at[n])
        for n, (source, target) in enumerate(
            [(ids_hbm, ids_ref), (states_hbm, states_ref), (gates_hbm, gates_ref), (gain_hbm, gain_ref)]
        )
    ]
    for copy in copies:
        copy.start()
    tokens = ids_ref.shape[1]
    own = lax.axis_index("tp") // SPLIT
    upper = lax.broadcasted_iota(jnp.int32, (tokens, tokens), 0)
    upper = (upper <= lax.broadcasted_iota(jnp.int32, (tokens, tokens), 1)).astype(F32).astype(BF16)
    slot = lax.broadcasted_iota(jnp.int32, (CAP, tokens), 0).astype(F32)
    copies[0].wait()
    picks = []
    for j in range(waves):
        target = lax.bitwise_xor(own, j) * (EXPERTS // NODES)
        matched = ids_ref[...] == target
        hit = jnp.sum(jnp.where(matched, 1.0, 0.0), axis=0, keepdims=True)
        hits = jnp.broadcast_to(hit, (CAP, tokens))
        place = jnp.dot(hits.astype(BF16), upper, preferred_element_type=F32) - 1.0
        picks.append(jnp.where((hits > 0.5) & (place == slot), 1.0, 0.0))
    for copy in copies[1:]:
        copy.wait()
    for j, picked in enumerate(picks):
        matched = ids_ref[...] == lax.bitwise_xor(own, j) * (EXPERTS // NODES)
        score = jnp.sum(jnp.where(matched, gates_ref[...], 0.0), axis=0, keepdims=True)
        weighted_ref[CAP * j : CAP * (j + 1), :] = picked * score
    picked = jnp.concatenate(picks, axis=0).astype(BF16)
    width = states_ref.shape[1]
    squares = 0.0
    for at in chunks(width):
        rows = jnp.dot(picked, states_ref[:, at], preferred_element_type=F32)
        rows_ref[:, at] = rows
        squares += jnp.sum(rows * rows, axis=1, keepdims=True)
    scale = lax.rsqrt(squares / width + EPSILON)
    for at in chunks(width):
        rows = rows_ref[:, at] * scale * gain_ref[:, at]
        for j, ref in enumerate(row_refs):
            ref[:, at] = rows[CAP * j : CAP * (j + 1)].astype(BF16)


def ready_kernel(ref, weighted_ref, out_ref, weights_ref):
    out_ref[...] = ref[...]
    weights = weighted_ref[...]
    high = weights.astype(BF16).astype(F32)
    weights_ref[...] = jnp.concatenate([high, weights - high, high], axis=0).T.astype(BF16)


def stack_kernel(*refs):
    for at in chunks(refs[-1].shape[1]):
        parts = [ref[:, at].astype(F32) for ref in refs[:-1]]
        refs[-1][:, at] = jnp.concatenate(parts, axis=0).astype(BF16)


def choose_kernel(even_ref, odd_ref, out_ref):
    even = lax.axis_index("tp") % 2 == 0

    @pl.when(even)
    def _():
        out_ref[...] = even_ref[...]

    @pl.when(jnp.logical_not(even))
    def _():
        out_ref[...] = odd_ref[...]


def mark_kernel(ref, out_ref):
    out_ref[...] = ref[:, :128].astype(F32)


def ffn_kernel(gate_ref, up_ref, down_ref, *refs):
    blocks, outs = refs[: len(refs) // 2], refs[len(refs) // 2 :]
    width = blocks[0].shape[1]
    gated = up = 0.0
    for at in chunks(width):
        both = jnp.concatenate([block[:, at] for block in blocks], axis=0)
        gated += jnp.dot(both, gate_ref[at, :], preferred_element_type=F32)
        up += jnp.dot(both, up_ref[at, :], preferred_element_type=F32)
    hidden = (gated / (1.0 + jnp.exp(-gated)) * up).astype(BF16)
    for at in chunks(width):
        result = jnp.dot(hidden, down_ref[:, at], preferred_element_type=F32)
        first = 0
        for out in outs:
            out[:, at] = result[first : first + out.shape[0]].astype(BF16)
            first += out.shape[0]


def rows_of(n):
    return slice(CAP * n, CAP * (n + 1))


def pair_kernel(first, home_ref, back_ref, *outs):
    for at in chunks(home_ref.shape[1]):
        total = home_ref[:, at].astype(F32) + back_ref[:, at].astype(F32)
        row = first
        for out in outs:
            out[:, at] = total[row : row + out.shape[0]].astype(out.dtype)
            row += out.shape[0]


def passed_kernel(first, home_ref, back_ref, more_ref, out_ref):
    for at in chunks(home_ref.shape[1]):
        total = home_ref[:, at].astype(F32) + back_ref[:, at].astype(F32)
        out_ref[:, at] = (total[first : first + CAP] + more_ref[:, at].astype(F32)).astype(BF16)


def total_kernel(*refs):
    arrays, outs = refs[:4], refs[4:]
    for at in chunks(arrays[0].shape[1]):
        total = sum(ref[:, at].astype(F32) for ref in arrays)
        for n, out in enumerate(outs):
            out[:, at] = total[rows_of(n)].astype(BF16)


def combine_kernel(weights_ref, *refs):
    near, others, (out_ref, held_ref, sems) = refs[:3], refs[3:-3], refs[-3:]
    weights = weights_ref[...]
    copies = []
    for n, at in enumerate(chunks(out_ref.shape[1], OUT_CHUNK)):
        own = sum(piece[:, at].astype(F32) for piece in near)
        rows = jnp.concatenate([own] + [piece[:, at].astype(F32) for piece in others], axis=0)
        high = rows.astype(BF16).astype(F32)
        rows = jnp.concatenate([high, high, rows - high], axis=0).astype(BF16)
        held_ref[:, at] = jnp.dot(weights, rows, preferred_element_type=F32).astype(BF16)
        copies.append(pltpu.make_async_copy(held_ref.at[:, at], out_ref.at[:, at], sems.at[n]))
        copies[-1].start()
    for copy in copies:
        copy.wait()


def local(states, norm_gain, w_gate, w_up, w_down, expert_ids, gate_weights):
    tokens, width = states.shape
    hid = w_gate.shape[1]
    devices = lax.axis_size("tp")
    waves = devices // SPLIT
    others = range(1, waves)

    def swap(x, mask):
        return lax.ppermute(x, "tp", [(i, i ^ mask[i % 2]) for i in range(devices)])

    def cross(x, j):
        return swap(x, (SPLIT * j + 4,) * 2)

    def shape(rows, columns, dtype=BF16):
        return jax.ShapeDtypeStruct((rows, columns), dtype)

    block = shape(CAP, width)

    def stack(pieces, after=()):
        rows = sum(x.shape[0] for x in pieces)
        return call(stack_kernel, shape(rows, width), pieces, after, moved=4 * rows * width)

    gain = norm_gain[None, :]
    ids, gates = expert_ids.T, gate_weights.T
    own, *away, weighted = call(
        functools.partial(pick_kernel, waves),
        [block] * waves + [shape(CAP * waves, tokens, F32)],
        [],
        far_args=[states, gain, ids, gates],
        scratch=[
            pltpu.VMEM((tokens, width), BF16),
            pltpu.VMEM((CAP * waves, width), F32),
            pltpu.VMEM((1, width), F32),
            pltpu.VMEM(ids.shape, ids.dtype),
            pltpu.VMEM(gates.shape, F32),
            pltpu.SemaphoreType.DMA((4,)),
        ],
        flops=2 * tokens * width * CAP * waves,
        moved=tokens * width * 2,
    )
    side_two = swap(own, SIDES[1])
    heads = [cross(away[j - 1], j) for j in others]
    own, weights = call(
        ready_kernel,
        [block, shape(tokens, 3 * CAP * waves)],
        [own, weighted],
        flops=OWN_FLOPS,
        moved=4 * CAP * width,
    )

    first = [own, swap(own, SIDES[0]), side_two]
    past = call(choose_kernel, block, [first[1], first[2]], moved=6 * CAP * width)
    past = swap(past, MIXED[0])
    rows = CAP * (waves - 1)
    far = heads[0] if waves == 2 else stack(heads)
    sent = [swap(far, s) for s in MIXED + (CORNER,)]
    marks = [call(mark_kernel, shape(CAP, 128, F32), [x]) for x in heads]
    early = stack(first + [far], after=marks)
    late = stack(sent + [past])
    blocks = [late, early, swap(late, OTHER), swap(early, OTHER)]
    late, early, late_away, early_away = call(
        ffn_kernel,
        [shape(*x.shape) for x in blocks],
        [w_gate, w_up, w_down] + blocks,
        flops=6 * sum(x.shape[0] for x in blocks) * width * hid,
        moved=6 * width * hid,
        limit=24,
    )

    def pair(home, back, first, outs, after=()):
        body = functools.partial(pair_kernel, CAP * first)
        moved = sum(6 * out.shape[0] * width for out in outs)
        return call(body, outs, [home, back], after, moved=moved)

    *sent, past = pair(late, swap(late_away, OTHER), 0, [shape(rows, width)] * 3 + [block])
    sent = [swap(x, s) for x, s in zip(sent, MIXED + (CORNER,))]
    past = swap(past, SIDES[0])
    back = swap(early_away, OTHER)
    (kept,) = pair(early, back, len(first), [shape(rows, width, F32)])
    totals = call(total_kernel, [block] * (waves - 1), [kept, sent[1], sent[0], sent[2]], moved=10 * rows * width)
    returned = [cross(totals[j - 1], j) for j in others]
    kept, one = pair(early, back, 0, [shape(CAP, width, F32), block], after=totals)
    body = functools.partial(passed_kernel, 2 * CAP)
    two = call(body, block, [early, back, past], after=[one], moved=10 * CAP * width)
    near = [kept, swap(one, SIDES[0]), swap(two, SIDES[1])]
    marks = [call(mark_kernel, shape(CAP, 128, F32), [x]) for x in returned]
    return call(
        combine_kernel,
        shape(tokens, width),
        [weights] + near + returned,
        after=marks,
        scratch=[pltpu.VMEM((tokens, width), BF16), pltpu.SemaphoreType.DMA((len(chunks(width, OUT_CHUNK)),))],
        out_kind=pl.ANY,
        flops=6 * tokens * width * CAP * waves,
        moved=tokens * width * 4,
    )


def solution(mesh):
    rows = P(("group", "tp"), None)
    in_specs = (rows, P(), P(None, "tp"), P(None, "tp"), P("tp", None), rows, rows)
    return jax.shard_map(local, mesh=mesh, in_specs=in_specs, out_specs=rows, check_vma=False)
```

```python
import functools

import jax
import jax.numpy as jnp
from jax import lax
from jax.experimental import pallas as pl
from jax.experimental.pallas import tpu as pltpu
from jax.sharding import PartitionSpec as P

EXPERTS = 256
NODES = 8
SPLIT = 8
CAP = 8
EPSILON = 1e-06
SIDES = ((2, 2), (4, 4))
MIXED = ((4, 2), (2, 4))
CORNER = (6, 6)
OTHER = (1, 1)
OWN_FLOPS = 7_000_000_000
CHUNK = 1024
OUT_CHUNK = 1792
F32 = jnp.float32
BF16 = jnp.bfloat16


def call(body, outs, args, after=(), far_args=(), scratch=(), flops=0, moved=0, limit=16, out_kind=pltpu.VMEM):
    left, used = len(far_args), len(far_args) + len(args)

    def run(*refs):
        body(*refs[:used], *refs[used + len(after) :])

    def space(kind):
        return pl.BlockSpec(memory_space=kind)

    far_args = [pltpu.with_memory_space_constraint(x, pltpu.HBM) for x in far_args]
    return pl.pallas_call(
        run,
        out_shape=outs,
        in_specs=[space(pltpu.HBM)] * left + [space(pltpu.VMEM)] * len(args) + [space(pl.ANY)] * len(after),
        out_specs=jax.tree.map(lambda _: space(out_kind), outs),
        scratch_shapes=list(scratch),
        compiler_params=pltpu.CompilerParams(vmem_limit_bytes=limit * 1024 * 1024),
        cost_estimate=pl.CostEstimate(flops=flops, bytes_accessed=moved, transcendentals=0),
    )(*far_args, *args, *after)


def chunks(width, size=CHUNK):
    return [slice(at, min(at + size, width)) for at in range(0, width, size)]


def pick_kernel(waves, states_hbm, gain_hbm, ids_hbm, gates_hbm, *refs):
    row_refs, weighted_ref = refs[:waves], refs[waves]
    states_ref, rows_ref, gain_ref, ids_ref, gates_ref, sems = refs[waves + 1 :]
    copies = [
        pltpu.make_async_copy(source, target, sems.at[n])
        for n, (source, target) in enumerate(
            [(ids_hbm, ids_ref), (states_hbm, states_ref), (gates_hbm, gates_ref), (gain_hbm, gain_ref)]
        )
    ]
    for copy in copies:
        copy.start()
    tokens = ids_ref.shape[1]
    own = lax.axis_index("tp") // SPLIT
    upper = lax.broadcasted_iota(jnp.int32, (tokens, tokens), 0)
    upper = (upper <= lax.broadcasted_iota(jnp.int32, (tokens, tokens), 1)).astype(F32).astype(BF16)
    slot = lax.broadcasted_iota(jnp.int32, (CAP, tokens), 0).astype(F32)
    copies[0].wait()
    picks = []
    for j in range(waves):
        target = lax.bitwise_xor(own, j) * (EXPERTS // NODES)
        matched = ids_ref[...] == target
        hit = jnp.sum(jnp.where(matched, 1.0, 0.0), axis=0, keepdims=True)
        hits = jnp.broadcast_to(hit, (CAP, tokens))
        place = jnp.dot(hits.astype(BF16), upper, preferred_element_type=F32) - 1.0
        picks.append(jnp.where((hits > 0.5) & (place == slot), 1.0, 0.0))
    for copy in copies[1:]:
        copy.wait()
    for j, picked in enumerate(picks):
        matched = ids_ref[...] == lax.bitwise_xor(own, j) * (EXPERTS // NODES)
        score = jnp.sum(jnp.where(matched, gates_ref[...], 0.0), axis=0, keepdims=True)
        weighted_ref[CAP * j : CAP * (j + 1), :] = picked * score
    picked = jnp.concatenate(picks, axis=0).astype(BF16)
    width = states_ref.shape[1]
    squares = 0.0
    for at in chunks(width):
        rows = jnp.dot(picked, states_ref[:, at], preferred_element_type=F32)
        rows_ref[:, at] = rows
        squares += jnp.sum(rows * rows, axis=1, keepdims=True)
    scale = lax.rsqrt(squares / width + EPSILON)
    for at in chunks(width):
        rows = rows_ref[:, at] * scale * gain_ref[:, at]
        for j, ref in enumerate(row_refs):
            ref[:, at] = rows[CAP * j : CAP * (j + 1)].astype(BF16)


def ready_kernel(ref, weighted_ref, out_ref, weights_ref):
    out_ref[...] = ref[...]
    weights = weighted_ref[...]
    high = weights.astype(BF16).astype(F32)
    weights_ref[...] = jnp.concatenate([high, weights - high, high], axis=0).T.astype(BF16)


def stack_kernel(*refs):
    for at in chunks(refs[-1].shape[1]):
        parts = [ref[:, at].astype(F32) for ref in refs[:-1]]
        refs[-1][:, at] = jnp.concatenate(parts, axis=0).astype(BF16)


def choose_kernel(even_ref, odd_ref, out_ref):
    even = lax.axis_index("tp") % 2 == 0

    @pl.when(even)
    def _():
        out_ref[...] = even_ref[...]

    @pl.when(jnp.logical_not(even))
    def _():
        out_ref[...] = odd_ref[...]


def mark_kernel(ref, out_ref):
    out_ref[...] = ref[:, :128].astype(F32)


def ffn_kernel(gate_ref, up_ref, down_ref, *refs):
    blocks, outs = refs[: len(refs) // 2], refs[len(refs) // 2 :]
    width = blocks[0].shape[1]
    gated = up = 0.0
    for at in chunks(width):
        both = jnp.concatenate([block[:, at] for block in blocks], axis=0)
        gated += jnp.dot(both, gate_ref[at, :], preferred_element_type=F32)
        up += jnp.dot(both, up_ref[at, :], preferred_element_type=F32)
    hidden = (gated / (1.0 + jnp.exp(-gated)) * up).astype(BF16)
    for at in chunks(width):
        result = jnp.dot(hidden, down_ref[:, at], preferred_element_type=F32)
        first = 0
        for out in outs:
            out[:, at] = result[first : first + out.shape[0]].astype(BF16)
            first += out.shape[0]


def rows_of(n):
    return slice(CAP * n, CAP * (n + 1))


def pair_kernel(first, home_ref, back_ref, *outs):
    for at in chunks(home_ref.shape[1]):
        total = home_ref[:, at].astype(F32) + back_ref[:, at].astype(F32)
        row = first
        for out in outs:
            out[:, at] = total[row : row + out.shape[0]].astype(out.dtype)
            row += out.shape[0]


def passed_kernel(first, home_ref, back_ref, more_ref, out_ref):
    for at in chunks(home_ref.shape[1]):
        total = home_ref[:, at].astype(F32) + back_ref[:, at].astype(F32)
        out_ref[:, at] = (total[first : first + CAP] + more_ref[:, at].astype(F32)).astype(BF16)


def total_kernel(*refs):
    arrays, outs = refs[:4], refs[4:]
    for at in chunks(arrays[0].shape[1]):
        total = sum(ref[:, at].astype(F32) for ref in arrays)
        for n, out in enumerate(outs):
            out[:, at] = total[rows_of(n)].astype(BF16)


def combine_kernel(weights_ref, *refs):
    near, others, (out_ref, held_ref, sems) = refs[:3], refs[3:-3], refs[-3:]
    weights = weights_ref[...]
    copies = []
    for n, at in enumerate(chunks(out_ref.shape[1], OUT_CHUNK)):
        own = sum(piece[:, at].astype(F32) for piece in near)
        rows = jnp.concatenate([own] + [piece[:, at].astype(F32) for piece in others], axis=0)
        high = rows.astype(BF16).astype(F32)
        rows = jnp.concatenate([high, high, rows - high], axis=0).astype(BF16)
        held_ref[:, at] = jnp.dot(weights, rows, preferred_element_type=F32).astype(BF16)
        copies.append(pltpu.make_async_copy(held_ref.at[:, at], out_ref.at[:, at], sems.at[n]))
        copies[-1].start()
    for copy in copies:
        copy.wait()


def local(states, norm_gain, w_gate, w_up, w_down, expert_ids, gate_weights):
    tokens, width = states.shape
    hid = w_gate.shape[1]
    devices = lax.axis_size("tp")
    waves = devices // SPLIT
    others = range(1, waves)

    def swap(x, mask):
        return lax.ppermute(x, "tp", [(i, i ^ mask[i % 2]) for i in range(devices)])

    def cross(x, j):
        return swap(x, (SPLIT * j + 4,) * 2)

    def shape(rows, columns, dtype=BF16):
        return jax.ShapeDtypeStruct((rows, columns), dtype)

    block = shape(CAP, width)

    def stack(pieces, after=()):
        rows = sum(x.shape[0] for x in pieces)
        return call(stack_kernel, shape(rows, width), pieces, after, moved=4 * rows * width)

    gain = norm_gain[None, :]
    ids, gates = expert_ids.T, gate_weights.T
    own, *away, weighted = call(
        functools.partial(pick_kernel, waves),
        [block] * waves + [shape(CAP * waves, tokens, F32)],
        [],
        far_args=[states, gain, ids, gates],
        scratch=[
            pltpu.VMEM((tokens, width), BF16),
            pltpu.VMEM((CAP * waves, width), F32),
            pltpu.VMEM((1, width), F32),
            pltpu.VMEM(ids.shape, ids.dtype),
            pltpu.VMEM(gates.shape, F32),
            pltpu.SemaphoreType.DMA((4,)),
        ],
        flops=2 * tokens * width * CAP * waves,
        moved=tokens * width * 2,
    )
    side_two = swap(own, SIDES[1])
    heads = [cross(away[j - 1], j) for j in others]
    own, weights = call(
        ready_kernel,
        [block, shape(tokens, 3 * CAP * waves)],
        [own, weighted],
        flops=OWN_FLOPS,
        moved=4 * CAP * width,
    )

    first = [own, swap(own, SIDES[0]), side_two]
    past = call(choose_kernel, block, [first[1], first[2]], moved=6 * CAP * width)
    past = swap(past, MIXED[0])
    rows = CAP * (waves - 1)
    far = heads[0] if waves == 2 else stack(heads)
    sent = [swap(far, s) for s in (CORNER,) + MIXED[::-1]]
    marks = [call(mark_kernel, shape(CAP, 128, F32), [x]) for x in heads]
    early = stack(first + [far], after=marks)
    late = stack(sent + [past])
    blocks = [late, early, swap(late, OTHER), swap(early, OTHER)]
    late, early, late_away, early_away = call(
        ffn_kernel,
        [shape(*x.shape) for x in blocks],
        [w_gate, w_up, w_down] + blocks,
        flops=6 * sum(x.shape[0] for x in blocks) * width * hid,
        moved=6 * width * hid,
        limit=24,
    )

    def pair(home, back, first, outs, after=()):
        body = functools.partial(pair_kernel, CAP * first)
        moved = sum(6 * out.shape[0] * width for out in outs)
        return call(body, outs, [home, back], after, moved=moved)

    *sent, past = pair(late, swap(late_away, OTHER), 0, [shape(rows, width)] * 3 + [block])
    sent = [swap(x, s) for x, s in zip(sent, (CORNER,) + MIXED[::-1])]
    past = swap(past, SIDES[0])
    back = swap(early_away, OTHER)
    (kept,) = pair(early, back, len(first), [shape(rows, width, F32)])
    totals = call(total_kernel, [block] * (waves - 1), [kept, sent[1], sent[2], sent[0]], moved=10 * rows * width)
    returned = [cross(totals[j - 1], j) for j in others]
    kept, one = pair(early, back, 0, [shape(CAP, width, F32), block], after=totals)
    body = functools.partial(passed_kernel, 2 * CAP)
    two = call(body, block, [early, back, past], after=[one], moved=10 * CAP * width)
    near = [kept, swap(one, SIDES[0]), swap(two, SIDES[1])]
    marks = [call(mark_kernel, shape(CAP, 128, F32), [x]) for x in returned]
    return call(
        combine_kernel,
        shape(tokens, width),
        [weights] + near + returned,
        after=marks,
        scratch=[pltpu.VMEM((tokens, width), BF16), pltpu.SemaphoreType.DMA((len(chunks(width, OUT_CHUNK)),))],
        out_kind=pl.ANY,
        flops=6 * tokens * width * CAP * waves,
        moved=tokens * width * 4,
    )


def solution(mesh):
    rows = P(("group", "tp"), None)
    in_specs = (rows, P(), P(None, "tp"), P(None, "tp"), P("tp", None), rows, rows)
    return jax.shard_map(local, mesh=mesh, in_specs=in_specs, out_specs=rows, check_vma=False)
```
